32 devices in a mesh: dp: 8 (over z, x), tensor: 4 (over y, core).
Axes of the slice: x: 2, y: 2, z: 4, core: 2. Of those that a mesh axis runs over, the one named last changes fastest.
Arguments:
- inputs: bfloat16 [2, 1024, 2560], P(None, 'dp'), may hold values from -6 to 6
- cotangent: bfloat16 [2, 1024, 2560], P(None, 'dp'), may hold values from -6 to 6
- prefix: int32 [2], replicated, may hold values from 102 to 512
- gain_attn: bfloat16 [2560], P('dp'), may hold values from 0.099609375 to 1.8984375
- w_query: bfloat16 [2560, 2560], P('dp', 'tensor'), may hold values from -0.15625 to 0.15625
- w_key: bfloat16 [2560, 640], P('dp', 'tensor'), may hold values from -0.15625 to 0.15625
- w_value: bfloat16 [2560, 640], P('dp', 'tensor'), may hold values from -0.125 to 0.125
- w_out: bfloat16 [2560, 2560], P('tensor', 'dp'), may hold values from -1 to 1
- gain_mlp: bfloat16 [2560], P('dp'), may hold values from 0.099609375 to 1.8984375
- w_gate: bfloat16 [2560, 7168], P('dp', 'tensor'), may hold values from -0.125 to 0.125
- w_up: bfloat16 [2560, 7168], P('dp', 'tensor'), may hold values from -0.125 to 0.125
- w_down: bfloat16 [7168, 2560], P('tensor', 'dp'), may hold values from -0.0625 to 0.0625
Outputs:
- result: float32 [2, 1024, 2560], P(None, 'dp')
- input_grad: float32 [2, 1024, 2560], P(None, 'dp')
- gain_attn_grad: float32 [2560], P('dp')
- w_query_grad: float32 [2560, 2560], P('dp', 'tensor')
- w_key_grad: float32 [2560, 640], P('dp', 'tensor')
- w_value_grad: float32 [2560, 640], P('dp', 'tensor')
- w_out_grad: float32 [2560, 2560], P('tensor', 'dp')
- gain_mlp_grad: float32 [2560], P('dp')
- w_gate_grad: float32 [2560, 7168], P('dp', 'tensor')
- w_up_grad: float32 [2560, 7168], P('dp', 'tensor')
- w_down_grad: float32 [7168, 2560], P('tensor', 'dp')
The draws below stay inside these ranges and needn't reach their ends.
Inputs may be any that keep to these rules, and one draw needn't show every extreme that they name: Every position of sequence s sees the first prefix[s] positions of that sequence.
All inputs are finite; a program needn't handle non-finite values.
Results may differ from the reference program's by a relative error of at most 0.014.
The reference program's roundings to bfloat16 on the way count: a program that leaves them out, or rounds other values in their place, can miss the bound.
Values may be sent and summed in bfloat16 or wider, within the bound.
No kernel may reach another device: no remote copies, remote signals or barrier semaphores. Data moves between devices by JAX's collectives and lax.ppermute only.
A program may use at most 176 MiB of HBM per device.

```python
import math
import jax
import jax.numpy as jnp
from jax import lax

D = 2560
HEADS = 32
KV_HEADS = 8
HEAD_DIM = 80
FF = 7168
ROWS = 128
SEQS = 2
LEN = 1024
N_DP = 8


def with_spikes(entries, key, source, target, blocks, factor):
    owner, partner = [(jnp.arange(entries.shape[dim]) // (entries.shape[dim] // blocks)).reshape([-1 if axis == dim else 1 for axis in range(entries.ndim)]) for dim in (source, target)]
    chosen = jax.random.permutation(key, blocks)[partner]
    strong = (owner == chosen) | (owner == (partner + blocks // 2) % blocks)
    return jnp.where(strong, factor * entries, entries)


def block_levels(own_key, shape, split, low, top_value):
    factor_of, own = 1.0, jax.random.fold_in(own_key, 6)
    for axis_at, parts in split:
        heights = jnp.exp(jax.random.uniform(jax.random.fold_in(own, axis_at), (parts,), jnp.float32, low / len(split), top_value / len(split)))
        factor_of = factor_of * jnp.repeat(heights, shape[axis_at] // parts).reshape([-1 if axis == axis_at else 1 for axis in range(len(shape))])
    return factor_of


def scatter_about(own_key, dims, deviation, bound, cuts=(), kind=jnp.bfloat16):
    drawn = deviation * jax.random.normal(own_key, dims, jnp.float32)
    if cuts:
        drawn = drawn * block_levels(own_key, dims, cuts, -0.22, 0.18)
    return jnp.clip(drawn, -bound, bound).astype(kind)


def gaussian_with(key, shape, spread, limit, pieces, heavy, held_as=jnp.bfloat16):
    values = spread * jax.random.normal(key, shape, jnp.float32)
    if pieces:
        values = values * block_levels(key, shape, pieces, -0.22, 0.18)
    return jnp.clip(with_spikes(values, jax.random.fold_in(key, 3), *heavy), -limit, limit).astype(held_as)


def setup_inputs(seed: int = 0) -> dict:
    key_list = jax.random.split(jax.random.key(seed), 13)
    return {
        "inputs": scatter_about(key_list[0], (SEQS, LEN, D), 1.0, 6.0, ((1, 8),)),
        "cotangent": gaussian_with(key_list[1], (SEQS, LEN, D), 1.0, 6.0, ((1, 8),), (1, 2, 8, 2.0)),
        "prefix": jax.random.randint(key_list[2], (SEQS,), ROWS * N_DP // 10, ROWS * N_DP // 2 + 1).astype(jnp.int32),
        "gain_attn": jnp.clip(1.0 + 0.18 * jax.random.normal(key_list[3], (D,), jnp.float32), 0.099609375, 1.8984375).astype(jnp.bfloat16),
        "w_query": scatter_about(key_list[4], (D, HEADS * HEAD_DIM), (D // 2) ** -0.5, 0.15625, ((0, 8), (1, 4))),
        "w_key": scatter_about(key_list[5], (D, KV_HEADS * HEAD_DIM), (D // 2) ** -0.5, 0.15625, ((0, 8), (1, 4))),
        "w_value": scatter_about(key_list[6], (D, KV_HEADS * HEAD_DIM), D ** -0.5, 0.125, ((0, 8), (1, 4))),
        "w_out": scatter_about(key_list[7], (HEADS * HEAD_DIM, D), (HEADS * HEAD_DIM // 64) ** -0.5, 1.0, ((0, 4), (1, 8))),
        "gain_mlp": jnp.clip(1.0 + 0.18 * jax.random.normal(key_list[8], (D,), jnp.float32), 0.099609375, 1.8984375).astype(jnp.bfloat16),
        "w_gate": scatter_about(key_list[9], (D, FF), D ** -0.5, 0.125, ((0, 8), (1, 4))),
        "w_up": scatter_about(key_list[10], (D, FF), D ** -0.5, 0.125, ((0, 8), (1, 4))),
        "w_down": scatter_about(key_list[11], (FF, D), FF ** -0.5, 0.0625, ((0, 4), (1, 8))),
    }


EPSILON = 1e-05
NEGATIVE = -1e+30
HIGHEST = lax.Precision.HIGHEST

@jax.custom_vjp
def low(v):
    return lax.optimization_barrier(v.astype(jnp.bfloat16)).astype(jnp.float32)

@jax.custom_vjp
def low_back(v):
    return v

def low_keep(v):
    return (low(v), None)

def low_pass(kept, grad):
    return (grad,)

def back_keep(v):
    return (v, None)

def back_low(kept, grad):
    return (low(grad),)
low.defvjp(low_keep, low_pass)
low_back.defvjp(back_keep, back_low)

def matmul(left, right):
    return jnp.dot(left, right, preferred_element_type=jnp.float32, precision=HIGHEST)

def rms_normed(values, gain):
    recip = lax.rsqrt(lax.optimization_barrier(jnp.mean(values * values, -1, keepdims=True)) + EPSILON)
    return values * recip * gain

def attend(queries, keys, values, prefix):
    seqs, length, kv_heads, group, head_dim = queries.shape
    block = math.gcd(length, 512)
    blocks = length // block
    scale = head_dim ** (-0.5)
    key_pos = jnp.arange(length, dtype=jnp.int32)

    def one_sequence(items):
        seq_queries, seq_keys, seq_values, seq_prefix = items

        def one_block(inner):
            block_queries, first = inner
            query_pos = first + jnp.arange(block, dtype=jnp.int32)
            scores = low_back(jnp.einsum('qkgd,tkd->kgqt', block_queries, seq_keys, precision=HIGHEST) * scale)
            allowed = (key_pos[None, :] <= query_pos[:, None]) | (key_pos[None, :] < seq_prefix)
            scores = jnp.where(allowed, scores, NEGATIVE)
            top = lax.optimization_barrier(jnp.max(scores, -1, keepdims=True))
            expo = jnp.exp(scores - top)
            probs = low(expo / lax.optimization_barrier(jnp.sum(expo, -1, keepdims=True)))
            return jnp.einsum('kgqt,tkd->qkgd', probs, seq_values, precision=HIGHEST)
        firsts = jnp.arange(blocks, dtype=jnp.int32) * block
        shaped = seq_queries.reshape(blocks, block, kv_heads, group, head_dim)
        mixed = lax.map(jax.checkpoint(one_block), (shaped, firsts))
        return mixed.reshape(length, kv_heads, group, head_dim)
    return lax.map(jax.checkpoint(one_sequence), (queries, keys, values, prefix))

def forward(inputs, gain_attn, w_query, w_key, w_value, w_out, gain_mlp, w_gate, w_up, w_down, prefix):
    seqs, length, width = inputs.shape
    flat = inputs.reshape(seqs * length, width)
    attn_in = low(rms_normed(flat, gain_attn))
    queries = low_back(low(matmul(attn_in, w_query)))
    keys = low_back(low(matmul(attn_in, w_key)))
    values = low_back(low(matmul(attn_in, w_value)))
    kv_heads = w_key.shape[1] // HEAD_DIM
    group = w_query.shape[1] // w_key.shape[1]
    mixed = attend(queries.reshape(seqs, length, kv_heads, group, HEAD_DIM), keys.reshape(seqs, length, kv_heads, HEAD_DIM), values.reshape(seqs, length, kv_heads, HEAD_DIM), prefix)
    heads = low_back(low(mixed.reshape(seqs * length, kv_heads * group * HEAD_DIM)))
    hidden = flat + low_back(matmul(heads, w_out))
    mlp_in = low(rms_normed(hidden, gain_mlp))
    gate = low_back(matmul(mlp_in, w_gate))
    up = low_back(matmul(mlp_in, w_up))
    product = low(jax.nn.silu(gate) * up)
    result = hidden + low_back(matmul(product, w_down))
    return result.reshape(seqs, length, width)

def reference(inputs, cotangent, prefix, gain_attn, w_query, w_key, w_value, w_out, gain_mlp, w_gate, w_up, w_down):
    floats = [item.astype(jnp.float32) for item in (inputs, gain_attn, w_query, w_key, w_value, w_out, gain_mlp, w_gate, w_up, w_down)]

    def wrapped(*items):
        return forward(*items, prefix)
    result, pullback = jax.vjp(wrapped, *floats)
    grads = pullback(cotangent.astype(jnp.float32))
    return (result, grads[0], grads[1], grads[2], grads[3], grads[4], grads[5], grads[6], grads[7], grads[8], grads[9])
```

```python
import jax
import jax.numpy as jnp
from jax import lax
from jax.sharding import PartitionSpec as P

HEAD_DIM = 80
EPSILON = 1e-05
NEGATIVE = -1e30
BF16 = jnp.bfloat16
F32 = jnp.float32
AXES = ("dp", "tensor")


def dot(left, right):
    return jnp.dot(left, right, preferred_element_type=F32)


def contract_last(left, right):
    return lax.dot_general(left, right, (((1,), (1,)), ((), ())), preferred_element_type=F32)


def contract_first(left, right):
    return lax.dot_general(left, right, (((0,), (0,)), ((), ())), preferred_element_type=F32)


def pick(stack, index):
    return lax.dynamic_index_in_dim(stack, index, 0, keepdims=False)


def place(parts, indices):
    total = jnp.zeros((len(parts),) + parts[0].shape, parts[0].dtype)
    for part, index in zip(parts, indices):
        total = lax.dynamic_update_index_in_dim(total, part, index, 0)
    return total


class Grid:
    def __init__(self, dp, tensor, seqs, kv_local):
        self.Y = seqs
        self.C = tensor // seqs
        self.U = kv_local
        self.Z = seqs * kv_local
        self.X = dp // self.Z
        assert self.C * self.Y == tensor and self.X * self.Z == dp
        i, j = lax.axis_index("dp"), lax.axis_index("tensor")
        self.z, self.x = i // self.X, i % self.X
        self.y, self.c = j // self.C, j % self.C
        order = list(range(0, self.Z, 2)) + list(range(1, self.Z, 2))[::-1]
        self.order = order
        self.ring = [order.index(z) for z in range(self.Z)]

    def move(self, value, target):
        pairs = []
        for z in range(self.Z):
            for x in range(self.X):
                for y in range(self.Y):
                    for c in range(self.C):
                        tz, tx, ty, tc = target(z, x, y, c)
                        here = ((z * self.X + x) * self.Y + y) * self.C + c
                        there = ((tz * self.X + tx) * self.Y + ty) * self.C + tc
                        pairs.append((here, there))
        return lax.ppermute(value, AXES, pairs)

    def to_z(self, value, k):
        return self.move(value, lambda z, x, y, c: ((z + k) % self.Z, x, y, c))

    def to_x(self, value, k):
        return self.move(value, lambda z, x, y, c: (z, (x + k) % self.X, y, c))

    def to_y(self, value, k):
        return self.move(value, lambda z, x, y, c: (z, x, (y + k) % self.Y, c))

    def to_c(self, value, k):
        return self.move(value, lambda z, x, y, c: (z, x, y, (c + k) % self.C))

    def along_ring(self, value, k):
        return self.move(
            value, lambda z, x, y, c: (self.order[(self.ring[z] + k) % self.Z], x, y, c)
        )

    def slot_z(self, s):
        place_of = jnp.array(self.ring, jnp.int32)[self.z]
        return jnp.array(self.order, jnp.int32)[(place_of - s) % self.Z]

    def gather_tokens(self, own):
        blocks = [own]
        for _ in range(self.Z - 1):
            blocks.append(self.along_ring(blocks[-1], 1))
        mine = jnp.concatenate(blocks, 0)
        return jnp.concatenate([mine] + [self.to_c(mine, k) for k in range(1, self.C)], 0)

    def scatter_tokens(self, partial):
        tokens = partial.shape[0] // self.C
        low = partial[tokens:].astype(BF16)
        mine = partial[:tokens]
        for h in range(1, self.C):
            part = low[(h - 1) * tokens : h * tokens]
            mine = mine + self.to_c(part, -h).astype(F32)
        own = tokens // self.Z
        total = mine[(self.Z - 1) * own :].astype(BF16)
        for s in range(self.Z - 2, -1, -1):
            total = self.along_ring(total, -1).astype(F32) + mine[s * own : (s + 1) * own]
            if s > 0:
                total = total.astype(BF16)
        return total

    def exchange_z(self, pick_for):
        parts = [pick_for(self.z)]
        for k in range(1, self.Z):
            parts.append(self.to_z(pick_for((self.z + k) % self.Z), k))
        return parts

    def from_z(self, k):
        return (self.z - k) % self.Z

    def spread_x(self, unit):
        parts = [unit] + [self.to_x(unit, k) for k in range(1, self.X)]
        return place(parts, [(self.x - k) % self.X for k in range(self.X)])

    def fetch_hidden(self, weight, x_first):
        rows, cols = weight.shape
        n = cols // self.Z
        pack = jnp.stack([weight[:, s * n : (s + 1) * n] for s in range(self.Z)], 0)
        parts = self.exchange_z(lambda zd: pick(pack, zd))
        unit = place(parts, [self.from_z(k) for k in range(self.Z)])

        def spread(value):
            return self.spread_x(value).transpose(1, 0, 2, 3).reshape(-1, n)

        if x_first:
            whole = spread(unit)
            return [whole] + [self.to_y(whole, k) for k in range(1, self.Y)]
        return [spread(unit)] + [spread(self.to_y(unit, k)) for k in range(1, self.Y)]

    def fetch_heads(self, packs, x_first):
        rows, n = packs[0].shape
        half = rows // self.Y
        pack = jnp.stack(packs, 0).reshape(self.U, self.Y, half, n).transpose(1, 0, 2, 3)
        near = [pick(pack, self.y)]
        for k in range(1, self.Y):
            near.append(self.to_y(pick(pack, (self.y + k) % self.Y), k))
        near = jnp.concatenate(near, 0)

        def for_z(zd):
            return pick(near, ((self.y - zd // self.U) % self.Y) * self.U + zd % self.U)

        parts = self.exchange_z(for_z)
        unit = place(parts, [self.from_z(k) for k in range(self.Z)])
        if x_first:
            unit = self.spread_x(unit)
            ys = [unit] + [self.to_y(unit, k) for k in range(1, self.Y)]
            both = place(ys, [(self.y - k) % self.Y for k in range(self.Y)])
            return both.transpose(2, 1, 0, 3, 4).reshape(-1, n)
        ys = [unit] + [self.to_y(unit, k) for k in range(1, self.Y)]
        unit = place(ys, [(self.y - k) % self.Y for k in range(self.Y)])
        both = self.spread_x(unit)
        return both.transpose(2, 0, 1, 3, 4).reshape(-1, n)

    def sum_x(self, total):
        out = pick(total, self.x).astype(F32)
        for k in range(1, self.X):
            out = out + self.to_x(pick(total, (self.x + k) % self.X), k).astype(F32)
        return out

    def return_hidden(self, grads, x_first):
        n = grads[0].shape[1]
        shaped = [
            g.reshape(self.Z, self.X, -1, n).transpose(1, 0, 2, 3) for g in grads
        ]
        if x_first:
            units = [self.sum_x(g) for g in shaped]
            total = units[0]
            for k in range(1, self.Y):
                total = total + self.to_y(units[k].astype(BF16), -k).astype(F32)
        else:
            total = shaped[0].astype(F32)
            for k in range(1, self.Y):
                total = total + self.to_y(shaped[k], -k).astype(F32)
            total = self.sum_x(total.astype(BF16))
        total = total.astype(BF16)
        parts = jnp.stack(self.exchange_z(lambda zd: pick(total, zd)), 0)
        return jnp.concatenate(
            [pick(parts, (self.z - s) % self.Z) for s in range(self.Z)], 1
        ).astype(F32)

    def return_heads(self, grad, x_first):
        n = grad.shape[1]
        shaped = grad.reshape(self.Z, self.X, self.Y, -1, n).transpose(2, 1, 0, 3, 4)
        total = pick(shaped, self.y).astype(F32)
        for k in range(1, self.Y):
            total = total + self.to_y(pick(shaped, (self.y + k) % self.Y), k).astype(F32)
        total = self.sum_x(total.astype(BF16)).astype(BF16)
        parts = jnp.stack(self.exchange_z(lambda zd: pick(total, zd)), 0)
        parts = jnp.stack([pick(parts, (self.z - s) % self.Z) for s in range(self.Z)], 0)
        parts = parts.reshape((self.Y, self.U) + parts.shape[1:])
        halves = [pick(parts, self.y)]
        for k in range(1, self.Y):
            halves.append(self.to_y(pick(parts, (self.y + k) % self.Y), k))
        rows = place(halves, [(self.y - k) % self.Y for k in range(self.Y)])
        return [rows[:, u].reshape(-1, n).astype(F32) for u in range(self.U)]

    def gather_gains(self, gains):
        xs = self.spread_x(gains)
        parts = [xs] + [self.to_z(xs, k) for k in range(1, self.Z)]
        whole = place(parts, [self.from_z(k) for k in range(self.Z)])
        return whole.transpose(2, 0, 1, 3).reshape(gains.shape[0], -1)

    def sum_gains(self, terms):
        number = terms.shape[0]
        part = terms
        for k in range(1, self.C):
            part = part + self.to_c(terms, k)
        terms = part
        for k in range(1, self.Y):
            part = part + self.to_y(terms, k)
        part = part.reshape(number, self.Z, self.X, -1).transpose(2, 1, 0, 3)
        out = pick(part, self.x)
        for k in range(1, self.X):
            out = out + self.to_x(pick(part, (self.x + k) % self.X), k)
        return sum(self.exchange_z(lambda zd: pick(out, zd)))

    def spread_rows(self, own):
        cs = [own] + [self.to_c(own, k) for k in range(1, self.C)]
        rows = place(cs, [(self.c - k) % self.C for k in range(self.C)])
        rows = rows.reshape(-1, own.shape[1])
        ys = [rows] + [self.to_y(rows, k) for k in range(1, self.Y)]
        return place(ys, [(self.y - k) % self.Y for k in range(self.Y)])


def per_device(
    dp,
    tensor,
    inputs,
    cotangent,
    prefix,
    gain_attn,
    w_query,
    w_key,
    w_value,
    w_out,
    gain_mlp,
    w_gate,
    w_up,
    w_down,
):
    seqs, rows, width = inputs.shape
    kv_local = w_key.shape[1] // HEAD_DIM
    group = w_query.shape[1] // w_key.shape[1]
    grid = Grid(dp, tensor, seqs, kv_local)
    own = rows // grid.C
    scale = HEAD_DIM ** (-0.5)
    q_cols = group * HEAD_DIM

    gains = grid.gather_gains(jnp.stack([gain_attn, gain_mlp], 0)).astype(F32)
    gain_one, gain_two = gains[0:1], gains[1:2]

    def heads_of(weight, u):
        size = weight.shape[1] // kv_local
        return weight[:, u * size : (u + 1) * size]

    w_qkv = grid.fetch_heads(
        [
            jnp.concatenate([heads_of(w_query, u), heads_of(w_key, u), heads_of(w_value, u)], 1)
            for u in range(kv_local)
        ],
        True,
    )
    w_out_t = w_out.T
    w_o = grid.fetch_heads([heads_of(w_out_t, u) for u in range(kv_local)], False)

    def own_rows(value):
        return lax.dynamic_slice(value, (grid.y, grid.c * own, 0), (1, own, width))[0]

    flat = own_rows(inputs).astype(F32)
    cot_own = own_rows(cotangent)
    recip_one = lax.rsqrt(jnp.mean(flat * flat, -1, keepdims=True) + EPSILON)
    normal_one = flat * recip_one
    attn_in = grid.gather_tokens((normal_one * gain_one).astype(BF16))

    w_g = grid.fetch_hidden(w_gate, True)
    w_u = grid.fetch_hidden(w_up, False)
    w_d = grid.fetch_hidden(w_down.T, True)
    mlp_grad = grid.gather_tokens(cot_own)

    qkv = dot(attn_in, w_qkv).astype(BF16)
    tokens = qkv.shape[0]
    queries = qkv[:, :q_cols].reshape(tokens, group, HEAD_DIM)
    kv_own = qkv[:, q_cols:]
    kv_all = jnp.concatenate([kv_own] + [grid.to_x(kv_own, k) for k in range(1, grid.X)], 0)
    keys, values = kv_all[:, :HEAD_DIM], kv_all[:, HEAD_DIM:]

    inner = lax.iota(jnp.int32, own)
    base = [
        grid.slot_z(s) * (grid.X * rows) + ((grid.c - h) % grid.C) * own
        for h in range(grid.C)
        for s in range(grid.Z)
    ]
    base = jnp.concatenate([b + inner for b in base])
    key_pos = jnp.concatenate([base + ((grid.x - k) % grid.X) * rows for k in range(grid.X)])
    query_pos = base + grid.x * rows
    seq_prefix = prefix[grid.y]
    allowed = (key_pos[None, :] <= query_pos[:, None]) | (key_pos[None, :] < seq_prefix)

    scores = jnp.einsum("qgd,td->gqt", queries, keys, preferred_element_type=F32) * scale
    scores = jnp.where(allowed[None], scores, NEGATIVE)
    top = jnp.max(scores, -1, keepdims=True)
    expo = jnp.exp(scores - top)
    probs = expo / jnp.sum(expo, -1, keepdims=True)
    probs_low = probs.astype(BF16)
    heads = (
        jnp.einsum("gqt,td->qgd", probs_low, values, preferred_element_type=F32)
        .astype(BF16)
        .reshape(tokens, -1)
    )
    attn_out = grid.scatter_tokens(contract_last(heads, w_o))
    hidden = flat + attn_out
    recip_two = lax.rsqrt(jnp.mean(hidden * hidden, -1, keepdims=True) + EPSILON)
    normal_two = hidden * recip_two
    mlp_in = grid.gather_tokens((normal_two * gain_two).astype(BF16))

    mlp_partial = 0.0
    in_partial = 0.0
    gate_grads, up_grads, products = [], [], []
    for wg, wu, wd in zip(w_g, w_u, w_d):
        gate = dot(mlp_in, wg)
        up = dot(mlp_in, wu)
        sigma = jax.nn.sigmoid(gate)
        product = (gate * sigma * up).astype(BF16)
        mlp_partial = mlp_partial + contract_last(product, wd)
        product_grad = dot(mlp_grad, wd)
        up_grad = (product_grad * gate * sigma).astype(BF16)
        gate_grad = (product_grad * up * sigma * (1.0 + gate * (1.0 - sigma))).astype(BF16)
        in_partial = in_partial + contract_last(gate_grad, wg) + contract_last(up_grad, wu)
        products.append(product)
        gate_grads.append(gate_grad)
        up_grads.append(up_grad)

    mlp_in_grad = grid.scatter_tokens(in_partial)
    result = grid.spread_rows(hidden + grid.scatter_tokens(mlp_partial))

    down_wgrad = grid.return_hidden(
        [contract_first(mlp_grad, p).astype(BF16) for p in products], True
    ).T
    gate_wgrad = grid.return_hidden(
        [contract_first(mlp_in, g).astype(BF16) for g in gate_grads], False
    )
    up_wgrad = grid.return_hidden(
        [contract_first(mlp_in, g).astype(BF16) for g in up_grads], True
    )

    out_grad = cot_own.astype(F32)
    scaled_two = mlp_in_grad * gain_two
    hidden_grad = out_grad + recip_two * (
        scaled_two - normal_two * jnp.mean(scaled_two * normal_two, -1, keepdims=True)
    )
    gain_two_term = jnp.sum(mlp_in_grad * normal_two, 0, keepdims=True)
    attn_grad = grid.gather_tokens(hidden_grad.astype(BF16))
    heads_grad = dot(attn_grad, w_o).astype(BF16)
    out_wgrad = grid.return_heads(contract_first(attn_grad, heads).astype(BF16), False)

    heads_grad = heads_grad.reshape(tokens, group, HEAD_DIM)
    prob_grad = jnp.einsum("qgd,td->gqt", heads_grad, values, preferred_element_type=F32)
    score_grad = (probs * (prob_grad - jnp.sum(probs * prob_grad, -1, keepdims=True))).astype(BF16)
    query_grad = jnp.einsum("gqt,td->qgd", score_grad, keys, preferred_element_type=F32) * scale
    key_parts = jnp.einsum("gqt,qgd->td", score_grad, queries, preferred_element_type=F32) * scale
    value_parts = jnp.einsum("gqt,qgd->td", probs_low, heads_grad, preferred_element_type=F32)
    kv_parts = jnp.concatenate([key_parts, value_parts], 1)
    kv_grad = kv_parts[:tokens]
    for k in range(1, grid.X):
        kv_grad = kv_grad + grid.to_x(kv_parts[k * tokens : (k + 1) * tokens], -k)
    qkv_grad = jnp.concatenate(
        [query_grad.astype(BF16).reshape(tokens, -1), kv_grad.astype(BF16)], 1
    )
    attn_in_grad = grid.scatter_tokens(contract_last(qkv_grad, w_qkv))
    qkv_wgrad = grid.return_heads(contract_first(attn_in, qkv_grad).astype(BF16), True)

    scaled_one = attn_in_grad * gain_one
    input_grad = hidden_grad + recip_one * (
        scaled_one - normal_one * jnp.mean(scaled_one * normal_one, -1, keepdims=True)
    )
    input_grad = grid.spread_rows(input_grad)
    gain_one_term = jnp.sum(attn_in_grad * normal_one, 0, keepdims=True)
    gain_sum = grid.sum_gains(jnp.concatenate([gain_one_term, gain_two_term], 0))

    return (
        result,
        input_grad,
        gain_sum[0],
        jnp.concatenate([w[:, :q_cols] for w in qkv_wgrad], 1),
        jnp.concatenate([w[:, q_cols : q_cols + HEAD_DIM] for w in qkv_wgrad], 1),
        jnp.concatenate([w[:, q_cols + HEAD_DIM :] for w in qkv_wgrad], 1),
        jnp.concatenate(out_wgrad, 1).T,
        gain_sum[1],
        gate_wgrad,
        up_wgrad,
        down_wgrad,
    )


def solution(mesh):
    dp, tensor = mesh.shape["dp"], mesh.shape["tensor"]

    def step(*args):
        return per_device(dp, tensor, *args)

    return jax.shard_map(
        step,
        mesh=mesh,
        in_specs=(
            P(None, "dp", None),
            P(None, "dp", None),
            P(),
            P("dp"),
            P("dp", "tensor"),
            P("dp", "tensor"),
            P("dp", "tensor"),
            P("tensor", "dp"),
            P("dp"),
            P("dp", "tensor"),
            P("dp", "tensor"),
            P("tensor", "dp"),
        ),
        out_specs=(
            P(None, "dp", None),
            P(None, "dp", None),
            P("dp"),
            P("dp", "tensor"),
            P("dp", "tensor"),
            P("dp", "tensor"),
            P("tensor", "dp"),
            P("dp"),
            P("dp", "tensor"),
            P("dp", "tensor"),
            P("tensor", "dp"),
        ),
        check_vma=False,
    )
```

```python
import functools

import jax
import jax.numpy as jnp
from jax import lax
from jax.experimental import pallas as pl
from jax.experimental.pallas import tpu as pltpu
from jax.sharding import PartitionSpec as P

HEAD_DIM = 80
EPSILON = 1e-05
NEGATIVE = -1e30
BF16 = jnp.bfloat16
F32 = jnp.float32
AXES = ("dp", "tensor")


def dot(left, right):
    return jnp.dot(left, right, preferred_element_type=F32)


def contract_last(left, right):
    return lax.dot_general(left, right, (((1,), (1,)), ((), ())), preferred_element_type=F32)


def contract_first(left, right):
    return lax.dot_general(left, right, (((0,), (0,)), ((), ())), preferred_element_type=F32)


def after(value, *others):
    return lax.optimization_barrier((value,) + others)[0]


def pick(stack, index):
    return lax.dynamic_index_in_dim(stack, index, 0, keepdims=False)


def place(parts, indices):
    total = jnp.zeros((len(parts),) + parts[0].shape, parts[0].dtype)
    for part, index in zip(parts, indices):
        total = lax.dynamic_update_index_in_dim(total, part, index, 0)
    return total


def whole_vmem():
    return pl.BlockSpec(memory_space=pltpu.VMEM)


def anywhere():
    return pl.BlockSpec(memory_space=pl.ANY)


class Taker:
    def __init__(self, refs):
        self.refs, self.at = refs, 0

    def __call__(self, number):
        taken = self.refs[self.at : self.at + number]
        self.at += number
        return taken


def pack_kernel(Z, where, gate, up, down, *outs):
    n = gate.shape[1] // Z
    for k in range(Z):
        wanted = lax.rem(where[0] + k, Z)
        for s in range(Z):

            @pl.when(wanted == s)
            def _(k=k, s=s):
                for i, weight in enumerate((gate, up, down)):
                    outs[k][:, i * n : (i + 1) * n] = weight[:, s * n : (s + 1) * n]


def pack_hidden(grid, w_gate, w_up, w_down_t):
    rows, cols = w_gate.shape
    return pl.pallas_call(
        functools.partial(pack_kernel, grid.Z),
        out_shape=[jax.ShapeDtypeStruct((rows, 3 * cols // grid.Z), BF16)] * grid.Z,
        in_specs=[pl.BlockSpec(memory_space=pltpu.SMEM)] + [whole_vmem()] * 3,
        out_specs=[whole_vmem()] * grid.Z,
        compiler_params=pltpu.CompilerParams(vmem_limit_bytes=32 * 2**20),
    )(grid.where, w_gate, w_up, w_down_t)


def unpack_kernel(Z, where, *refs):
    parts, outs = refs[:Z], refs[Z:]
    n = parts[0].shape[1] // 3
    for k in range(Z):
        block = lax.rem(where[0] - k + Z, Z)
        for s in range(Z):

            @pl.when(block == s)
            def _(k=k, s=s):
                for i in range(3):
                    outs[i][:, s * n : (s + 1) * n] = parts[k][:, i * n : (i + 1) * n].astype(F32)


def unpack_hidden(grid, parts):
    rows, n = parts[0].shape
    return pl.pallas_call(
        functools.partial(unpack_kernel, grid.Z),
        out_shape=[jax.ShapeDtypeStruct((rows, grid.Z * n // 3), F32)] * 3,
        in_specs=[pl.BlockSpec(memory_space=pltpu.SMEM)] + [whole_vmem()] * grid.Z,
        out_specs=[whole_vmem()] * 3,
        compiler_params=pltpu.CompilerParams(vmem_limit_bytes=32 * 2**20),
    )(grid.where, *parts)


def pack_heads_kernel(U, Y, sizes, where, *refs):
    take = Taker(refs)
    sources, outs, weights, sems = take(len(sizes)), take(Y), take(len(sizes)), take(1)[0]
    copies = [
        pltpu.make_async_copy(source, weight, sems.at[i])
        for i, (source, weight) in enumerate(zip(sources, weights))
    ]
    for copy in copies:
        copy.start()
    for copy in copies:
        copy.wait()
    half = outs[0].shape[1]
    y = where[2]
    for u in range(U):
        first = 0
        for weight, size in zip(weights, sizes):
            columns = weight[:, u * size : (u + 1) * size].astype(F32)
            for k in range(Y):
                part = columns[:half]
                for h in range(1, Y):
                    chosen = lax.rem(y + k, Y) == h
                    part = jnp.where(chosen, columns[h * half : (h + 1) * half], part)
                outs[k][u, :, first : first + size] = part.astype(BF16)
            first += size
        spare = outs[0].shape[2] - first
        if spare:
            for k in range(Y):
                outs[k][u, :, first:] = jnp.zeros((half, spare), BF16)


def pack_heads(grid, weights):
    U, Y = grid.U, grid.Y
    rows = weights[0].shape[0]
    sizes = tuple(weight.shape[1] // U for weight in weights)
    n = -(-sum(sizes) // 128) * 128
    return pl.pallas_call(
        functools.partial(pack_heads_kernel, U, Y, sizes),
        out_shape=[jax.ShapeDtypeStruct((U, rows // Y, n), BF16)] * Y,
        in_specs=[pl.BlockSpec(memory_space=pltpu.SMEM)] + [anywhere()] * len(weights),
        out_specs=[whole_vmem()] * Y,
        scratch_shapes=[pltpu.VMEM(weight.shape, BF16) for weight in weights]
        + [pltpu.SemaphoreType.DMA((len(weights),))],
        compiler_params=pltpu.CompilerParams(vmem_limit_bytes=32 * 2**20),
    )(grid.where, *weights)


def route_kernel(Z, U, Y, where, *refs):
    near, outs = refs[:Y], refs[Y:]
    z, y = where[0], where[2]
    for k in range(Z):
        target = lax.rem(z + k, Z)
        u = lax.rem(target, U)
        from_y = lax.rem(y - lax.div(target, U) + Y, Y)
        for r in range(Y):

            @pl.when(from_y == r)
            def _(k=k, r=r, u=u):
                outs[k][...] = near[r][u]


def route_heads(grid, near):
    _, half, n = near[0].shape
    return pl.pallas_call(
        functools.partial(route_kernel, grid.Z, grid.U, grid.Y),
        out_shape=[jax.ShapeDtypeStruct((half, n), BF16)] * grid.Z,
        in_specs=[pl.BlockSpec(memory_space=pltpu.SMEM)] + [whole_vmem()] * grid.Y,
        out_specs=[whole_vmem()] * grid.Z,
        compiler_params=pltpu.CompilerParams(vmem_limit_bytes=32 * 2**20),
    )(grid.where, *near)


def assemble_kernel(Z, X, Y, where, *refs):
    units, out = refs[: X * Y], refs[X * Y]
    z, x, y = where[0], where[1], where[2]
    for yr in range(Y):
        for xr in range(X):
            for k in range(Z):
                spot = lax.rem(z - k + Z, Z) * X + lax.rem(x - xr + X, X)
                spot = spot * Y + lax.rem(y - yr + Y, Y)
                out[spot] = units[yr * X + xr][k]


def assemble(grid, units):
    Z, X, Y = grid.Z, grid.X, grid.Y
    _, part, n = units[0].shape
    out = pl.pallas_call(
        functools.partial(assemble_kernel, Z, X, Y),
        out_shape=jax.ShapeDtypeStruct((Z * X * Y, part, n), BF16),
        in_specs=[pl.BlockSpec(memory_space=pltpu.SMEM)] + [whole_vmem()] * (X * Y),
        out_specs=whole_vmem(),
        compiler_params=pltpu.CompilerParams(vmem_limit_bytes=32 * 2**20),
    )(grid.where, *units)
    return out.reshape(-1, n)


def hidden_kernel(Z, X, tiles, order, where, *refs):
    take = Taker(refs)
    act_refs, grad_refs, units = take(tiles), take(tiles), take(X * Z)
    in_own, in_low, out_own, out_low, both_grads, products = take(6)
    weights, acts, grads, sems = take(4)
    z, x = where[0], where[1]
    rows = units[0].shape[0]
    n = units[0].shape[1] // 3
    tokens = act_refs[0].shape[0]
    own = tokens // Z
    ring = sum(jnp.where(z == value, place, 0) for place, value in enumerate(order))

    def rows_of(s):
        ranked = lax.rem(ring - s + Z, Z)
        at = sum(jnp.where(ranked == place, value, 0) for place, value in enumerate(order))
        return at * own

    copies = []
    for xr in range(X):
        for k in range(Z):
            spot = lax.rem(z - k + Z, Z) * X + lax.rem(x - xr + X, X)
            at = pl.ds(pl.multiple_of(spot * rows, 16), rows)
            copies.append(pltpu.make_async_copy(units[xr * Z + k], weights.at[at], sems.at[0]))
    for i in range(tiles):
        copies.append(pltpu.make_async_copy(act_refs[i], acts.at[i], sems.at[0]))
        for s in range(Z):
            at = pl.ds(pl.multiple_of(rows_of(s), own), own)
            copies.append(
                pltpu.make_async_copy(
                    grad_refs[i].at[at], grads.at[i, pl.ds(s * own, own)], sems.at[0]
                )
            )
    for copy in copies:
        copy.start()
    for copy in copies:
        copy.wait()

    def one_tile(i, carry):
        both = dot(acts[i], weights[:, : 2 * n])
        gate, up = both[:, :n], both[:, n:]
        product_grad = dot(grads[i], weights[:, 2 * n :])
        sigma = 1.0 / (1.0 + jnp.exp(-gate))
        silu = gate * sigma
        product = (silu * up).astype(BF16)
        up_grad = (product_grad * silu).astype(BF16)
        gate_grad = (product_grad * up * sigma * (1.0 + gate * (1.0 - sigma))).astype(BF16)
        both_grad = jnp.concatenate([gate_grad, up_grad], 1)
        at = pl.ds(pl.multiple_of(i * tokens, tokens), tokens)
        both_grads[at, :] = both_grad
        in_part = contract_last(both_grad, weights[:, : 2 * n])
        out_part = contract_last(product, weights[:, 2 * n :])
        for s in range(Z):
            spot = pl.ds(pl.multiple_of(i * tokens + rows_of(s), own), own)
            products[spot, :] = product[s * own : (s + 1) * own]

        @pl.when(i == 0)
        def _():
            in_own[...] = in_part
            for s in range(Z):
                spot = pl.ds(pl.multiple_of(rows_of(s), own), own)
                out_own[spot, :] = out_part[s * own : (s + 1) * own]

        @pl.when(i > 0)
        def _():
            low_at = pl.ds(pl.multiple_of((i - 1) * tokens, tokens), tokens)
            in_low[low_at, :] = in_part.astype(BF16)
            for s in range(Z):
                spot = pl.ds(pl.multiple_of((i - 1) * tokens + rows_of(s), own), own)
                out_low[spot, :] = out_part[s * own : (s + 1) * own].astype(BF16)

        return carry

    lax.fori_loop(0, tiles, one_tile, 0)


def hidden_layer(grid, acts, grads, units):
    Z, X, C = grid.Z, grid.X, grid.C
    tokens, width = acts[0].shape
    n = units[0].shape[1] // 3
    shape = jax.ShapeDtypeStruct
    rows = [shape((tokens, width), F32), shape(((C - 1) * tokens, width), BF16)]
    shapes = rows + rows + [shape((C * tokens, 2 * n), BF16), shape((C * tokens, n), BF16)]
    return pl.pallas_call(
        functools.partial(hidden_kernel, Z, X, C, tuple(grid.order)),
        out_shape=shapes,
        in_specs=[pl.BlockSpec(memory_space=pltpu.SMEM)] + [anywhere()] * (2 * C + X * Z),
        out_specs=[whole_vmem()] * len(shapes),
        scratch_shapes=[
            pltpu.VMEM((width, 3 * n), BF16),
            pltpu.VMEM((C, tokens, width), BF16),
            pltpu.VMEM((C, tokens, width), BF16),
            pltpu.SemaphoreType.DMA((1,)),
        ],
        compiler_params=pltpu.CompilerParams(vmem_limit_bytes=36 * 2**20),
        cost_estimate=pl.CostEstimate(
            flops=12 * C * tokens * width * n,
            bytes_accessed=20 * 2**20,
            transcendentals=C * tokens * n,
        ),
    )(grid.where, *acts, *grads, *units)


def norm_kernel(values, more, gain, total, normed):
    hidden = values[...].astype(F32) + more[...].astype(F32)
    recip = lax.rsqrt(jnp.mean(hidden * hidden, -1, keepdims=True) + EPSILON)
    total[...] = hidden
    normed[...] = (hidden * recip * gain[...]).astype(BF16)


def add_norm(values, more, gain):
    return pl.pallas_call(
        norm_kernel,
        out_shape=[
            jax.ShapeDtypeStruct(values.shape, F32),
            jax.ShapeDtypeStruct(values.shape, BF16),
        ],
        in_specs=[whole_vmem()] * 3,
        out_specs=[whole_vmem()] * 2,
        compiler_params=pltpu.CompilerParams(vmem_limit_bytes=32 * 2**20),
    )(values, more, gain)


def norm_back_kernel(number, *refs):
    parts = refs[:number]
    values, beside, gain, grad, low, gain_term = refs[number:]
    part = parts[0][...].astype(F32)
    for ref in parts[1:]:
        part = part + ref[...].astype(F32)
    value = values[...].astype(F32)
    recip = lax.rsqrt(jnp.mean(value * value, -1, keepdims=True) + EPSILON)
    normal = value * recip
    scaled = part * gain[...]
    mean = jnp.mean(scaled * normal, -1, keepdims=True)
    total = beside[...].astype(F32) + recip * (scaled - normal * mean)
    grad[...] = total
    low[...] = total.astype(BF16)
    gain_term[...] = jnp.sum(part * normal, 0, keepdims=True)


def norm_back(parts, values, beside, gain):
    return pl.pallas_call(
        functools.partial(norm_back_kernel, len(parts)),
        out_shape=[
            jax.ShapeDtypeStruct(values.shape, F32),
            jax.ShapeDtypeStruct(values.shape, BF16),
            jax.ShapeDtypeStruct(gain.shape, F32),
        ],
        in_specs=[whole_vmem()] * (3 + len(parts)),
        out_specs=[whole_vmem()] * 3,
        compiler_params=pltpu.CompilerParams(vmem_limit_bytes=32 * 2**20),
    )(*parts, values, beside, gain)


def place_kernel(Y, C, where, *refs):
    parts, out = refs[:-1], refs[-1]
    y, c = where[2], where[3]
    own = parts[0].shape[0]
    for i, part in enumerate(parts):
        at = lax.rem(c - i // Y + C, C) * own
        at = pl.ds(pl.multiple_of(at, own), own)
        out[lax.rem(y - i % Y + Y, Y), at, :] = part[...].astype(F32)


def place_rows(grid, parts):
    own, width = parts[0].shape
    return pl.pallas_call(
        functools.partial(place_kernel, grid.Y, grid.C),
        out_shape=jax.ShapeDtypeStruct((grid.Y, grid.C * own, width), F32),
        in_specs=[pl.BlockSpec(memory_space=pltpu.SMEM)] + [whole_vmem()] * len(parts),
        out_specs=whole_vmem(),
        compiler_params=pltpu.CompilerParams(vmem_limit_bytes=32 * 2**20),
    )(grid.where, *parts)


def core_sum_kernel(number, own, *refs):
    lows, outs = refs[:number], refs[number:]
    total = own[...]
    for low in lows:
        total = total + low[...].astype(F32)
    if len(outs) == 1:
        outs[0][...] = total.astype(outs[0].dtype)
        return
    half = total.shape[0] // 2
    outs[0][...] = total[:half].astype(outs[0].dtype)
    outs[1][...] = total[half:].astype(outs[1].dtype)


def core_sum(own, lows, kind, pieces):
    rows, width = own.shape
    return pl.pallas_call(
        functools.partial(core_sum_kernel, len(lows)),
        out_shape=[jax.ShapeDtypeStruct((rows // pieces, width), kind)] * pieces,
        in_specs=[whole_vmem()] * (1 + len(lows)),
        out_specs=[whole_vmem()] * pieces,
        compiler_params=pltpu.CompilerParams(vmem_limit_bytes=32 * 2**20),
    )(own, *lows)


def hidden_weight_kernel(X, tiles, where, *refs):
    take = Taker(refs)
    acts, grads = take(tiles), take(tiles)
    Y = (len(refs) - 2 * tiles - X - 1) // 2
    both_grads, products, outs, total = take(Y), take(Y), take(X), take(1)[0]
    x = where[1]
    tokens = acts[0].shape[0]
    rows = outs[0].shape[0]
    n = products[0].shape[1]

    def summed(parts, values):
        sums = None
        for i in range(tiles):
            at = i // Y * tokens
            part = contract_first(parts[i][...], values[i % Y][at : at + tokens, :])
            sums = part if sums is None else sums + part
        return sums

    total[:, : 2 * n] = summed(acts, both_grads)
    total[:, 2 * n :] = summed(grads, products)
    for xr in range(X):
        at = pl.ds(pl.multiple_of(lax.rem(x + xr, X) * rows, 8), rows)
        outs[xr][...] = total[at, :].astype(BF16)


def hidden_weight_grad(grid, k, acts, grads, both_grads, products):
    Z, X, tiles = grid.Z, grid.X, len(acts)
    tokens, width = acts[0].shape
    n = products[0].shape[1]
    block = width // Z

    def features(i, s):
        return (0, lax.rem(s[0] + k, Z))

    return pl.pallas_call(
        functools.partial(hidden_weight_kernel, X, tiles),
        out_shape=[jax.ShapeDtypeStruct((block // X, 3 * n), BF16)] * X,
        grid_spec=pltpu.PrefetchScalarGridSpec(
            num_scalar_prefetch=1,
            grid=(1,),
            in_specs=[pl.BlockSpec((tokens, block), features)] * (2 * tiles)
            + [pl.BlockSpec(value.shape, lambda i, s: (0, 0)) for value in both_grads + products],
            out_specs=[pl.BlockSpec((block // X, 3 * n), lambda i, s: (0, 0))] * X,
            scratch_shapes=[pltpu.VMEM((block, 3 * n), F32)],
        ),
        compiler_params=pltpu.CompilerParams(vmem_limit_bytes=26 * 2**20),
        cost_estimate=pl.CostEstimate(
            flops=6 * tiles * tokens * block * n, bytes_accessed=10 * 2**20, transcendentals=0
        ),
    )(grid.where, *acts, *grads, *both_grads, *products)


def weight_kernel(X, Y, where, act, grad, *refs):
    outs, total = refs[: Y * X], refs[Y * X]
    x, y = where[1], where[2]
    part = outs[0].shape[1]
    total[...] = contract_first(act[...], grad[...])
    for xr in range(X):
        for yr in range(Y):
            at = (lax.rem(x + xr, X) * Y + lax.rem(y + yr, Y)) * part
            at = pl.ds(pl.multiple_of(at, 8), part)
            outs[yr * X + xr][0] = total[at, :].astype(BF16)


def weight_grad(grid, act, grad):
    Z, X, Y = grid.Z, grid.X, grid.Y
    tokens, width = act.shape
    n = grad.shape[1]
    part = width // (Z * X * Y)
    return pl.pallas_call(
        functools.partial(weight_kernel, X, Y),
        out_shape=[jax.ShapeDtypeStruct((Z, part, n), BF16)] * (Y * X),
        grid_spec=pltpu.PrefetchScalarGridSpec(
            num_scalar_prefetch=1,
            grid=(Z,),
            in_specs=[
                pl.BlockSpec((tokens, width // Z), lambda k, s: (0, lax.rem(s[0] + k, Z))),
                pl.BlockSpec((tokens, n), lambda k, s: (0, 0)),
            ],
            out_specs=[pl.BlockSpec((1, part, n), lambda k, s: (k, 0, 0))] * (Y * X),
            scratch_shapes=[pltpu.VMEM((width // Z, n), F32)],
        ),
        compiler_params=pltpu.CompilerParams(vmem_limit_bytes=26 * 2**20),
        cost_estimate=pl.CostEstimate(
            flops=2 * tokens * width * n, bytes_accessed=2 * width * n, transcendentals=0
        ),
    )(grid.where, act, grad)


def identity(number):
    row = lax.broadcasted_iota(jnp.int32, (number, number), 0)
    column = lax.broadcasted_iota(jnp.int32, (number, number), 1)
    return jnp.where(row == column, 1.0, 0.0).astype(BF16)


def visible(X, rows, where, limit, first, tile, keys):
    x = where[1]
    key = lax.broadcasted_iota(jnp.int32, (keys, 1), 0)
    tokens = keys // X
    inside = lax.rem(key, tokens)
    key_x = lax.rem(x - lax.div(key, tokens) + X, X)
    key_pos = (lax.div(inside, rows) * X + key_x) * rows + lax.rem(inside, rows)
    query = first + lax.broadcasted_iota(jnp.int32, (1, tile), 1)
    query_pos = (lax.div(query, rows) * X + x) * rows + lax.rem(query, rows)
    return (key_pos <= query_pos) | (key_pos < limit)


def split_heads(qkv, others, queries, keys_values, turned, group):
    tokens = qkv.shape[0]
    for g in range(group):
        queries[g] = qkv[:, g * HEAD_DIM : (g + 1) * HEAD_DIM]
    eye = identity(2 * HEAD_DIM)
    for i in range(1 + len(others)):
        at = slice(i * tokens, (i + 1) * tokens)
        both = qkv[:, group * HEAD_DIM : (group + 2) * HEAD_DIM] if i == 0 else others[i - 1][...]
        keys_values[0, at, :] = both[:, :HEAD_DIM]
        keys_values[1, at, :] = both[:, HEAD_DIM:]
        turned[:, at] = contract_last(eye, both).astype(BF16)


def attend_kernel(X, rows, group, tile, where, prefix, qkv, *refs):
    take = Taker(refs)
    others, heads, stats = take(X - 1), take(1)[0], take(1)[0]
    queries, keys_values, turned = take(3)
    tokens = qkv.shape[0]
    scale = HEAD_DIM ** (-0.5)
    split_heads(qkv, others, queries, keys_values, turned, group)
    limit = prefix[where[2]]
    for t in range(tokens // tile):
        at = slice(t * tile, (t + 1) * tile)
        allowed = visible(X, rows, where, limit, t * tile, tile, X * tokens)
        outs = []
        for g in range(group):
            scores = contract_last(keys_values[0], queries[g, at, :]) * scale
            scores = jnp.where(allowed, scores, NEGATIVE)
            top = jnp.max(scores, 0, keepdims=True)
            expo = jnp.exp(scores - top)
            total = jnp.sum(expo, 0, keepdims=True)
            probs = (expo / total).astype(BF16)
            outs.append(jnp.transpose(dot(turned[HEAD_DIM:, :], probs)).astype(BF16))
            stats[g : g + 1, at] = top
            stats[group + g : group + g + 1, at] = total
        heads[at, :] = jnp.concatenate(outs, 1)


def attend_back_kernel(X, rows, group, tile, where, prefix, qkv, *refs):
    take = Taker(refs)
    others, heads_grad, stats = take(X - 1), take(1)[0], take(1)[0]
    query_grad, kv_grads = take(1)[0], take(X)
    queries, keys_values, turned, grads, key_sum, value_sum = take(6)
    tokens = qkv.shape[0]
    scale = HEAD_DIM ** (-0.5)
    split_heads(qkv, others, queries, keys_values, turned, group)
    for g in range(group):
        grads[g] = heads_grad[:, g * HEAD_DIM : (g + 1) * HEAD_DIM]
    limit = prefix[where[2]]
    for t in range(tokens // tile):
        at = slice(t * tile, (t + 1) * tile)
        allowed = visible(X, rows, where, limit, t * tile, tile, X * tokens)
        outs = []
        for g in range(group):
            query, grad = queries[g, at, :], grads[g, at, :]
            scores = contract_last(keys_values[0], query) * scale
            scores = jnp.where(allowed, scores, NEGATIVE)
            probs = jnp.exp(scores - stats[g : g + 1, at]) / stats[group + g : group + g + 1, at]
            prob_grad = contract_last(keys_values[1], grad)
            mean = jnp.sum(probs * prob_grad, 0, keepdims=True)
            score_grad = (probs * (prob_grad - mean)).astype(BF16)
            out = jnp.transpose(dot(turned[:HEAD_DIM, :], score_grad)) * scale
            outs.append(out.astype(BF16))
            key_part = dot(score_grad, query)
            value_part = dot(probs.astype(BF16), grad)
            if t == 0 and g == 0:
                key_sum[...] = key_part
                value_sum[...] = value_part
            else:
                key_sum[...] += key_part
                value_sum[...] += value_part
        query_grad[at, :] = jnp.concatenate(outs, 1)
    for i, out in enumerate(kv_grads):
        at = slice(i * tokens, (i + 1) * tokens)
        out[:, :HEAD_DIM] = key_sum[at, :] * scale
        out[:, HEAD_DIM:] = value_sum[at, :]


def query_tile(tokens, keys):
    tile = tokens
    while tile > 128 and tile * keys > 2**19:
        tile = tile // 2
    return tile


def attend(grid, rows, group, prefix, qkv, others):
    tokens, keys = qkv.shape[0], grid.X * qkv.shape[0]
    smem = pl.BlockSpec(memory_space=pltpu.SMEM)
    return pl.pallas_call(
        functools.partial(attend_kernel, grid.X, rows, group, query_tile(tokens, keys)),
        out_shape=[
            jax.ShapeDtypeStruct((tokens, group * HEAD_DIM), BF16),
            jax.ShapeDtypeStruct((2 * group, tokens), F32),
        ],
        in_specs=[smem, smem] + [whole_vmem()] * grid.X,
        out_specs=[whole_vmem()] * 2,
        scratch_shapes=[
            pltpu.VMEM((group, tokens, HEAD_DIM), BF16),
            pltpu.VMEM((2, keys, HEAD_DIM), BF16),
            pltpu.VMEM((2 * HEAD_DIM, keys), BF16),
        ],
        compiler_params=pltpu.CompilerParams(vmem_limit_bytes=36 * 2**20),
        cost_estimate=pl.CostEstimate(
            flops=8 * group * tokens * keys * 128,
            bytes_accessed=4 * 2**20,
            transcendentals=group * tokens * keys,
        ),
    )(grid.where, prefix, qkv, *others)


def attend_back(grid, rows, group, prefix, qkv, others, heads_grad, stats):
    tokens, keys = qkv.shape[0], grid.X * qkv.shape[0]
    smem = pl.BlockSpec(memory_space=pltpu.SMEM)
    return pl.pallas_call(
        functools.partial(attend_back_kernel, grid.X, rows, group, query_tile(tokens, keys)),
        out_shape=[jax.ShapeDtypeStruct((tokens, group * HEAD_DIM), BF16)]
        + [jax.ShapeDtypeStruct((tokens, 2 * HEAD_DIM), F32)] * grid.X,
        in_specs=[smem, smem] + [whole_vmem()] * (grid.X + 2),
        out_specs=[whole_vmem()] * (1 + grid.X),
        scratch_shapes=[
            pltpu.VMEM((group, tokens, HEAD_DIM), BF16),
            pltpu.VMEM((2, keys, HEAD_DIM), BF16),
            pltpu.VMEM((2 * HEAD_DIM, keys), BF16),
            pltpu.VMEM((group, tokens, HEAD_DIM), BF16),
            pltpu.VMEM((keys, HEAD_DIM), F32),
            pltpu.VMEM((keys, HEAD_DIM), F32),
        ],
        compiler_params=pltpu.CompilerParams(vmem_limit_bytes=36 * 2**20),
        cost_estimate=pl.CostEstimate(
            flops=16 * group * tokens * keys * 128,
            bytes_accessed=4 * 2**20,
            transcendentals=group * tokens * keys,
        ),
    )(grid.where, prefix, qkv, *others, heads_grad, stats)


class Grid:
    def __init__(self, dp, tensor, seqs, kv_local):
        self.Y = seqs
        self.C = tensor // seqs
        self.U = kv_local
        self.Z = seqs * kv_local
        self.X = dp // self.Z
        assert self.C * self.Y == tensor and self.X * self.Z == dp
        i, j = lax.axis_index("dp"), lax.axis_index("tensor")
        self.z, self.x = i // self.X, i % self.X
        self.y, self.c = j // self.C, j % self.C
        self.where = jnp.stack([self.z, self.x, self.y, self.c]).astype(jnp.int32)
        order = list(range(0, self.Z, 2)) + list(range(1, self.Z, 2))[::-1]
        self.order = order
        self.ring = [order.index(z) for z in range(self.Z)]

    def move(self, value, target):
        pairs = []
        for z in range(self.Z):
            for x in range(self.X):
                for y in range(self.Y):
                    for c in range(self.C):
                        tz, tx, ty, tc = target(z, x, y, c)
                        here = ((z * self.X + x) * self.Y + y) * self.C + c
                        there = ((tz * self.X + tx) * self.Y + ty) * self.C + tc
                        pairs.append((here, there))
        return lax.ppermute(value, AXES, pairs)

    def to_z(self, value, k):
        return self.move(value, lambda z, x, y, c: ((z + k) % self.Z, x, y, c))

    def hop_z(self, value, k):
        if 1 < k < self.Z - 1:
            return self.to_z(self.to_z(value, 1), k - 1)
        return self.to_z(value, k)

    def to_x(self, value, k):
        return self.move(value, lambda z, x, y, c: (z, (x + k) % self.X, y, c))

    def to_y(self, value, k):
        return self.move(value, lambda z, x, y, c: (z, x, (y + k) % self.Y, c))

    def to_c(self, value, k):
        return self.move(value, lambda z, x, y, c: (z, x, y, (c + k) % self.C))

    def along_ring(self, value, k):
        return self.move(
            value, lambda z, x, y, c: (self.order[(self.ring[z] + k) % self.Z], x, y, c)
        )

    def slot_z(self, s):
        place_of = sum(jnp.where(self.z == z, ring, 0) for z, ring in enumerate(self.ring))
        place_of = (place_of - s) % self.Z
        return sum(jnp.where(place_of == at, z, 0) for at, z in enumerate(self.order))

    def to_xy(self, value, kx, ky):
        return self.move(
            value, lambda z, x, y, c: (z, (x + kx) % self.X, (y + ky) % self.Y, c)
        )

    def groups(self, names):
        sizes = {"z": self.Z, "x": self.X, "y": self.Y, "c": self.C}
        members = {}
        for z in range(self.Z):
            for x in range(self.X):
                for y in range(self.Y):
                    for c in range(self.C):
                        at = {"z": z, "x": x, "y": y, "c": c}
                        key = tuple(at[name] for name in sizes if name not in names)
                        rank = 0
                        for name in names:
                            rank = rank * sizes[name] + at[name]
                        index = ((z * self.X + x) * self.Y + y) * self.C + c
                        members.setdefault(key, {})[rank] = index
        return [[group[rank] for rank in range(len(group))] for group in members.values()]

    def gather(self, own, names):
        return lax.all_gather(own, AXES, axis=0, tiled=True, axis_index_groups=self.groups(names))

    def scatter(self, partial, names):
        return lax.psum_scatter(
            partial,
            AXES,
            scatter_dimension=0,
            tiled=True,
            axis_index_groups=self.groups(names),
        )

    def ring_steps(self, own, steps):
        blocks = [own]
        for _ in range(steps):
            blocks.append(self.along_ring(blocks[-1], 1))
        return blocks

    def spread_yc(self, mine):
        pieces = [mine] + [self.to_y(mine, k) for k in range(1, self.Y)]
        return pieces + [self.to_c(piece, k) for k in range(1, self.C) for piece in pieces]

    def gather_wide(self, blocks, hold=()):
        half = self.Z // 2
        first = jnp.concatenate(blocks[:half], 0)
        second = jnp.concatenate(blocks[half:], 0)
        pieces = [jnp.concatenate([first, second], 0)]
        for k in range(1, self.Y):
            pieces.append(
                jnp.concatenate([after(self.to_y(first, k), *hold), self.to_y(second, k)], 0)
            )
        return pieces + [self.to_c(piece, k) for k in range(1, self.C) for piece in pieces]

    def ring_sum(self, slots, holds=()):
        total = slots[-1].astype(BF16)
        for i, s in enumerate(range(self.Z - 2, -1, -1)):
            if i < len(holds):
                total = after(total, *holds[i])
            arrived = self.along_ring(total, -1)
            total = arrived.astype(F32) + slots[s]
            if s > 0:
                total = total.astype(BF16)
        return arrived, slots[0]

    def exchange_z(self, parts):
        return [parts[0]] + [self.to_z(parts[k], k) for k in range(1, self.Z)]

    def spread_xy(self, unit):
        return [
            unit if xr == yr == 0 else self.to_xy(unit, xr, yr)
            for yr in range(self.Y)
            for xr in range(self.X)
        ]

    def send_xy(self, units):
        return [
            unit if i == 0 else self.to_xy(unit, i % self.X, i // self.X)
            for i, unit in enumerate(units)
        ]

    def sum_xy(self, arrived):
        sums = []
        for k in range(self.Z):
            total = arrived[0][k].astype(F32)
            for unit in arrived[1:]:
                total = total + unit[k].astype(F32)
            sums.append(total.astype(BF16))
        return sums

    def return_heads(self, units):
        parts = jnp.stack(self.exchange_z(self.sum_xy(units)), 0)
        parts = jnp.stack([pick(parts, (self.z - s) % self.Z) for s in range(self.Z)], 0)
        parts = parts.reshape((self.Y, self.U) + parts.shape[1:])
        halves = [pick(parts, self.y)]
        for k in range(1, self.Y):
            halves.append(self.to_y(pick(parts, (self.y + k) % self.Y), k))
        rows = place(halves, [(self.y - k) % self.Y for k in range(self.Y)])
        return [rows[:, u].reshape(-1, rows.shape[3]) for u in range(self.U)]

    def from_z(self, k):
        return (self.z - k) % self.Z

    def spread_x(self, unit):
        parts = [unit] + [self.to_x(unit, k) for k in range(1, self.X)]
        return place(parts, [(self.x - k) % self.X for k in range(self.X)])

    def gather_gains(self, gains):
        xs = self.spread_x(gains)
        parts = [xs] + [self.to_z(xs, k) for k in range(1, self.Z)]
        whole = place(parts, [self.from_z(k) for k in range(self.Z)])
        return whole.transpose(2, 0, 1, 3).reshape(gains.shape[0], -1)

    def sum_gains(self, terms):
        number = terms.shape[0]
        part = terms
        for k in range(1, self.C):
            part = part + self.to_c(terms, k)
        terms = part
        for k in range(1, self.Y):
            part = part + self.to_y(terms, k)
        part = part.reshape(number, self.Z, self.X, -1).transpose(2, 1, 0, 3)
        out = pick(part, self.x)
        for k in range(1, self.X):
            out = out + self.to_x(pick(part, (self.x + k) % self.X), k)
        return sum(self.exchange_z([pick(out, (self.z + k) % self.Z) for k in range(self.Z)]))


def per_device(
    dp,
    tensor,
    inputs,
    cotangent,
    prefix,
    gain_attn,
    w_query,
    w_key,
    w_value,
    w_out,
    gain_mlp,
    w_gate,
    w_up,
    w_down,
):
    seqs, rows, width = inputs.shape
    kv_local = w_key.shape[1] // HEAD_DIM
    group = w_query.shape[1] // w_key.shape[1]
    grid = Grid(dp, tensor, seqs, kv_local)
    own = rows // grid.C
    q_cols = group * HEAD_DIM

    def own_rows(value):
        return lax.dynamic_slice(value, (grid.y, grid.c * own, 0), (1, own, width))[0]

    others = range(1, grid.X)
    middle = grid.Z // 2
    ends = [k for k in range(1, grid.Z) if k != middle]
    near = pack_heads(grid, [w_query, w_key, w_value])
    near_own = near[0]
    near = [near_own] + [grid.to_y(near[k], k) for k in range(1, grid.Y)]
    gains = grid.gather_gains(jnp.stack([gain_attn, gain_mlp], 0))
    cot_own = own_rows(cotangent)
    cot_all = grid.gather(cot_own, "z")
    flat = own_rows(inputs)
    gain_one, gain_two = gains[0:1].astype(F32), gains[1:2].astype(F32)
    values = flat.astype(F32)
    recip = lax.rsqrt(jnp.mean(values * values, -1, keepdims=True) + EPSILON)
    attn_own = after((values * recip * gain_one).astype(BF16), *near)
    attn_in = grid.gather(attn_own, "zc")
    qkv_parts = grid.exchange_z(route_heads(grid, near))

    packed = pack_hidden(grid, after(w_gate, attn_own), w_up, w_down.T)
    out_near = pack_heads(grid, [after(w_out.T, packed[0])])
    out_near = [out_near[0]] + [grid.to_y(out_near[k], k) for k in range(1, grid.Y)]

    def ring_on(blocks, *hold):
        return blocks + [grid.along_ring(after(blocks[-1], *hold), 1)]

    qkv_units = grid.spread_xy(after(jnp.stack(qkv_parts, 0), cot_all, *out_near))
    out_parts = route_heads(grid, [after(part, *qkv_parts) for part in out_near])
    out_parts = grid.exchange_z(out_parts)
    arrived, first = {0: packed[0]}, out_parts[1:]
    for k in [middle] + ends:
        arrived[k] = grid.hop_z(after(packed[k], *first), k)
        first = [arrived[k]]
    w_qkv = assemble(grid, [after(u, *out_parts[1:]) for u in qkv_units])[:, : q_cols + 2 * HEAD_DIM]
    qkv = dot(attn_in, w_qkv).astype(BF16)
    tokens = qkv.shape[0]
    kv_own = qkv[:, q_cols:]
    kv_others = [grid.to_x(kv_own, k) for k in others]
    heads, stats = attend(grid, rows, group, prefix, qkv, kv_others)
    moved_x, first = {}, qkv_units[1:]
    for k in [0, middle] + ends:
        moved_x[k] = [grid.to_x(after(arrived[k], *first), x) for x in others]
        first = moved_x[k]
        if k == 0:
            out_unit = after(jnp.stack(out_parts, 0), *kv_others, *first)
            out_units = grid.spread_xy(out_unit)
            w_o = assemble(grid, out_units)[:, :q_cols]
            first = out_units[1:]
    mlp_grad = grid.spread_yc(after(cot_all, *out_units[1:]))
    attn_partial = contract_last(after(heads, arrived[middle]), w_o).astype(BF16)
    attn_out = grid.scatter(attn_partial, "zc")
    held = mlp_grad[: grid.Y] + [arrived[ends[0]]] + moved_x[middle]
    hidden, mlp_own = add_norm(flat, after(attn_out, *held), gain_two)
    mlp_blocks = ring_on([mlp_own])
    mlp_blocks = ring_on(mlp_blocks, *mlp_grad, *moved_x[ends[0]])
    for _ in range(grid.Z - 3):
        mlp_blocks = ring_on(mlp_blocks, arrived[ends[-1]])
    mlp_in = grid.gather_wide(mlp_blocks, moved_x[ends[-1]])
    units = [arrived[k] for k in range(grid.Z)]
    units = units + [moved_x[k][x - 1] for x in others for k in range(grid.Z)]

    layers, in_moved, hold = [None] * grid.Y, [], ()
    for yr in range(grid.Y - 1, -1, -1):
        acts = [mlp_in[c * grid.Y + yr] for c in range(grid.C)]
        acts[0] = after(acts[0], *hold)
        grads = [mlp_grad[c * grid.Y + yr] for c in range(grid.C)]
        layers[yr] = hidden_layer(grid, acts, grads, units)
        each = acts[0].shape[0]
        half = each // 2
        low = after(layers[yr][1], *[sent[0] for sent in in_moved])
        moved = [grid.to_c(low[(h - 1) * each : h * each], -h) for h in range(1, grid.C)]
        if yr > 0:
            hold = core_sum(layers[yr][0], moved, BF16, 2)
            in_moved.append([grid.to_y(hold[1], -yr), grid.to_y(hold[0], -yr)])
    both_grads = [layer[4] for layer in layers]
    products = [layer[5] for layer in layers]

    order = [middle] + ends + [0]
    swapped, hidden_parts, holds = [], [None] * grid.Z, []
    for at, k in enumerate(order):
        hold = [in_late] if at else []
        given = both_grads[:-1] + [after(both_grads[-1], *hold)]
        parts = list(hidden_weight_grad(grid, k, mlp_in, mlp_grad, given, products))
        if at == 0:
            in_late, in_first = core_sum(after(layers[0][0], *parts), moved, F32, 2)
        first = swapped[-1] if swapped else []
        swapped.append([grid.to_x(after(parts[xr], *first), xr) for xr in others])
        holds.append(parts)
        hidden_parts[k] = core_sum(parts[0], swapped[-1], BF16, 1)[0]
    for sent in in_moved:
        in_first = in_first + sent[0].astype(F32)
    in_late = after(in_late, in_first)
    for sent in in_moved:
        in_late = in_late + sent[1].astype(F32)
    slots = [
        (in_late, in_first)[2 * s // grid.Z][s % (grid.Z // 2) * own :][:own]
        for s in range(grid.Z)
    ]
    holds, last = [[], holds[1], holds[2] + [hidden_parts[middle]]], holds[3]
    in_parts = grid.ring_sum(slots, holds)
    hidden_grad, hidden_low, gain_two_term = norm_back(in_parts, hidden, cot_own, gain_two)
    attn_grad = grid.gather(hidden_low, "zc")
    out_y = []
    for yr in range(grid.Y - 1, -1, -1):
        low = after(layers[yr][3], in_parts[0])
        moved = [grid.to_c(low[(h - 1) * each : h * each], -h) for h in range(1, grid.C)]
        if yr > 0:
            out_sum = core_sum(layers[yr][2], moved, BF16, 1)[0]
            out_y.append(grid.to_y(out_sum, -yr))
    arrived, first = list(hidden_parts), []
    for k in order[:-1]:
        arrived[k] = grid.hop_z(after(hidden_parts[k], *first), k)
        first = [arrived[k]]
    attn_grad = after(attn_grad, arrived[middle], *last, *swapped[2], *out_y)
    out_sum = core_sum(layers[0][2], moved + out_y, BF16, 1)[0]
    mlp_out = grid.scatter(after(out_sum, attn_grad), "z")
    heads_grad = dot(attn_grad, w_o).astype(BF16)
    out_units = weight_grad(grid, attn_grad, heads)

    heads_grad = after(heads_grad, *out_units)
    query_grad, *kv_parts = attend_back(
        grid, rows, group, prefix, qkv, kv_others, heads_grad, stats
    )
    kv_moved = [grid.to_x(kv_parts[k], -k) for k in others]
    kv_grad = kv_parts[0]
    for part in kv_moved:
        kv_grad = kv_grad + part
    qkv_grad = jnp.concatenate(
        [query_grad, kv_grad.astype(BF16)], 1
    )
    qkv_grad = after(qkv_grad, arrived[order[1]], *swapped[3])
    attn_in_grad = grid.scatter(contract_last(qkv_grad, w_qkv).astype(BF16), "zc")
    qkv_moved = grid.send_xy(weight_grad(grid, attn_in, qkv_grad))
    out_moved = grid.send_xy([after(unit, *qkv_moved[1:]) for unit in out_units])
    ready = after(attn_in_grad, arrived[order[2]], *qkv_moved[1:])
    _, input_low, gain_one_term = norm_back([ready], flat, hidden_grad, gain_one)
    rows_y = [input_low] + [grid.to_y(input_low, k) for k in range(1, grid.Y)]
    rows_c = [grid.to_c(part, k) for k in range(1, grid.C) for part in rows_y]
    input_grad = place_rows(grid, rows_y + rows_c)
    gain_sum = grid.sum_gains(jnp.concatenate([gain_one_term, gain_two_term], 0))

    out_wgrad = grid.return_heads([after(unit, *rows_y[1:]) for unit in out_moved])
    qkv_wgrad = grid.return_heads([after(unit, input_low) for unit in qkv_moved])
    gate_wgrad, up_wgrad, down_wgrad = unpack_hidden(
        grid, [after(a, *qkv_moved[1:]) for a in arrived]
    )
    down_wgrad = down_wgrad.T
    result = hidden + mlp_out.astype(F32)
    result = grid.gather(after(result, attn_in_grad), "yc").reshape(seqs, rows, width)

    return (
        result,
        input_grad,
        gain_sum[0],
        jnp.concatenate([w[:, :q_cols] for w in qkv_wgrad], 1).astype(F32),
        jnp.concatenate([w[:, q_cols : q_cols + HEAD_DIM] for w in qkv_wgrad], 1).astype(F32),
        jnp.concatenate([w[:, q_cols + HEAD_DIM :] for w in qkv_wgrad], 1).astype(F32),
        jnp.concatenate(out_wgrad, 1).T.astype(F32),
        gain_sum[1],
        gate_wgrad,
        up_wgrad,
        down_wgrad,
    )


def solution(mesh):
    dp, tensor = mesh.shape["dp"], mesh.shape["tensor"]

    def step(*args):
        return per_device(dp, tensor, *args)

    return jax.shard_map(
        step,
        mesh=mesh,
        in_specs=(
            P(None, "dp", None),
            P(None, "dp", None),
            P(),
            P("dp"),
            P("dp", "tensor"),
            P("dp", "tensor"),
            P("dp", "tensor"),
            P("tensor", "dp"),
            P("dp"),
            P("dp", "tensor"),
            P("dp", "tensor"),
            P("tensor", "dp"),
        ),
        out_specs=(
            P(None, "dp", None),
            P(None, "dp", None),
            P("dp"),
            P("dp", "tensor"),
            P("dp", "tensor"),
            P("dp", "tensor"),
            P("tensor", "dp"),
            P("dp"),
            P("dp", "tensor"),
            P("dp", "tensor"),
            P("tensor", "dp"),
        ),
        check_vma=False,
    )
```

```python
import functools

import jax
import jax.numpy as jnp
from jax import lax
from jax.experimental import pallas as pl
from jax.experimental.pallas import tpu as pltpu
from jax.sharding import PartitionSpec as P

HEAD_DIM = 80
EPSILON = 1e-05
NEGATIVE = -1e30
BF16 = jnp.bfloat16
F32 = jnp.float32
AXES = ("dp", "tensor")


def dot(left, right):
    return jnp.dot(left, right, preferred_element_type=F32)


def contract_last(left, right):
    return lax.dot_general(left, right, (((1,), (1,)), ((), ())), preferred_element_type=F32)


def contract_first(left, right):
    return lax.dot_general(left, right, (((0,), (0,)), ((), ())), preferred_element_type=F32)


def after(value, *others):
    return lax.optimization_barrier((value,) + others)[0]


def pick(stack, index):
    return lax.dynamic_index_in_dim(stack, index, 0, keepdims=False)


def place(parts, indices):
    total = jnp.zeros((len(parts),) + parts[0].shape, parts[0].dtype)
    for part, index in zip(parts, indices):
        total = lax.dynamic_update_index_in_dim(total, part, index, 0)
    return total


def whole_vmem():
    return pl.BlockSpec(memory_space=pltpu.VMEM)


def anywhere():
    return pl.BlockSpec(memory_space=pl.ANY)


class Taker:
    def __init__(self, refs):
        self.refs, self.at = refs, 0

    def __call__(self, number):
        taken = self.refs[self.at : self.at + number]
        self.at += number
        return taken


def pack_kernel(Z, where, gate, up, down, *outs):
    n = gate.shape[1] // Z
    for k in range(Z):
        wanted = lax.rem(where[0] + k, Z)
        for s in range(Z):

            @pl.when(wanted == s)
            def _(k=k, s=s):
                for i, weight in enumerate((gate, up, down)):
                    outs[k][:, i * n : (i + 1) * n] = weight[:, s * n : (s + 1) * n]


def pack_hidden(grid, w_gate, w_up, w_down_t):
    rows, cols = w_gate.shape
    return pl.pallas_call(
        functools.partial(pack_kernel, grid.Z),
        out_shape=[jax.ShapeDtypeStruct((rows, 3 * cols // grid.Z), BF16)] * grid.Z,
        in_specs=[pl.BlockSpec(memory_space=pltpu.SMEM)] + [whole_vmem()] * 3,
        out_specs=[whole_vmem()] * grid.Z,
        compiler_params=pltpu.CompilerParams(vmem_limit_bytes=32 * 2**20),
    )(grid.where, w_gate, w_up, w_down_t)


def unpack_kernel(Z, where, *refs):
    parts, outs = refs[:Z], refs[Z:]
    n = parts[0].shape[1] // 3
    for k in range(Z):
        block = lax.rem(where[0] - k + Z, Z)
        for s in range(Z):

            @pl.when(block == s)
            def _(k=k, s=s):
                for i in range(3):
                    outs[i][:, s * n : (s + 1) * n] = parts[k][:, i * n : (i + 1) * n].astype(F32)


def unpack_hidden(grid, parts):
    rows, n = parts[0].shape
    return pl.pallas_call(
        functools.partial(unpack_kernel, grid.Z),
        out_shape=[jax.ShapeDtypeStruct((rows, grid.Z * n // 3), F32)] * 3,
        in_specs=[pl.BlockSpec(memory_space=pltpu.SMEM)] + [whole_vmem()] * grid.Z,
        out_specs=[whole_vmem()] * 3,
        compiler_params=pltpu.CompilerParams(vmem_limit_bytes=32 * 2**20),
    )(grid.where, *parts)


def pack_heads_kernel(U, Y, sizes, where, *refs):
    take = Taker(refs)
    sources, outs, weights, sems = take(len(sizes)), take(Y), take(len(sizes)), take(1)[0]
    copies = [
        pltpu.make_async_copy(source, weight, sems.at[i])
        for i, (source, weight) in enumerate(zip(sources, weights))
    ]
    for copy in copies:
        copy.start()
    for copy in copies:
        copy.wait()
    half = outs[0].shape[1]
    y = where[2]
    for u in range(U):
        first = 0
        for weight, size in zip(weights, sizes):
            columns = weight[:, u * size : (u + 1) * size].astype(F32)
            for k in range(Y):
                part = columns[:half]
                for h in range(1, Y):
                    chosen = lax.rem(y + k, Y) == h
                    part = jnp.where(chosen, columns[h * half : (h + 1) * half], part)
                outs[k][u, :, first : first + size] = part.astype(BF16)
            first += size
        spare = outs[0].shape[2] - first
        if spare:
            for k in range(Y):
                outs[k][u, :, first:] = jnp.zeros((half, spare), BF16)


def pack_heads(grid, weights):
    U, Y = grid.U, grid.Y
    rows = weights[0].shape[0]
    sizes = tuple(weight.shape[1] // U for weight in weights)
    n = -(-sum(sizes) // 128) * 128
    return pl.pallas_call(
        functools.partial(pack_heads_kernel, U, Y, sizes),
        out_shape=[jax.ShapeDtypeStruct((U, rows // Y, n), BF16)] * Y,
        in_specs=[pl.BlockSpec(memory_space=pltpu.SMEM)] + [anywhere()] * len(weights),
        out_specs=[whole_vmem()] * Y,
        scratch_shapes=[pltpu.VMEM(weight.shape, BF16) for weight in weights]
        + [pltpu.SemaphoreType.DMA((len(weights),))],
        compiler_params=pltpu.CompilerParams(vmem_limit_bytes=32 * 2**20),
    )(grid.where, *weights)


def route_kernel(Z, U, Y, where, *refs):
    near, outs = refs[:Y], refs[Y:]
    z, y = where[0], where[2]
    for k in range(Z):
        target = lax.rem(z + k, Z)
        u = lax.rem(target, U)
        from_y = lax.rem(y - lax.div(target, U) + Y, Y)
        for r in range(Y):

            @pl.when(from_y == r)
            def _(k=k, r=r, u=u):
                outs[k][...] = near[r][u]


def route_heads(grid, near):
    _, half, n = near[0].shape
    return pl.pallas_call(
        functools.partial(route_kernel, grid.Z, grid.U, grid.Y),
        out_shape=[jax.ShapeDtypeStruct((half, n), BF16)] * grid.Z,
        in_specs=[pl.BlockSpec(memory_space=pltpu.SMEM)] + [whole_vmem()] * grid.Y,
        out_specs=[whole_vmem()] * grid.Z,
        compiler_params=pltpu.CompilerParams(vmem_limit_bytes=32 * 2**20),
    )(grid.where, *near)


def assemble_kernel(Z, X, Y, where, *refs):
    units, out = refs[: X * Y], refs[X * Y]
    z, x, y = where[0], where[1], where[2]
    for yr in range(Y):
        for xr in range(X):
            for k in range(Z):
                spot = lax.rem(z - k + Z, Z) * X + lax.rem(x - xr + X, X)
                spot = spot * Y + lax.rem(y - yr + Y, Y)
                out[spot] = units[yr * X + xr][k]


def assemble(grid, units):
    Z, X, Y = grid.Z, grid.X, grid.Y
    _, part, n = units[0].shape
    out = pl.pallas_call(
        functools.partial(assemble_kernel, Z, X, Y),
        out_shape=jax.ShapeDtypeStruct((Z * X * Y, part, n), BF16),
        in_specs=[pl.BlockSpec(memory_space=pltpu.SMEM)] + [whole_vmem()] * (X * Y),
        out_specs=whole_vmem(),
        compiler_params=pltpu.CompilerParams(vmem_limit_bytes=32 * 2**20),
    )(grid.where, *units)
    return out.reshape(-1, n)


def hidden_kernel(Z, X, tiles, order, where, *refs):
    take = Taker(refs)
    act_refs, grad_refs, units = take(tiles), take(tiles), take(X * Z)
    in_own, in_low, out_own, out_low, both_grads, products = take(6)
    weights, acts, grads, sems = take(4)
    z, x = where[0], where[1]
    rows = units[0].shape[0]
    n = units[0].shape[1] // 3
    tokens = act_refs[0].shape[0]
    own = tokens // Z
    ring = sum(jnp.where(z == value, place, 0) for place, value in enumerate(order))

    def rows_of(s):
        ranked = lax.rem(ring - s + Z, Z)
        at = sum(jnp.where(ranked == place, value, 0) for place, value in enumerate(order))
        return at * own

    copies = []
    for xr in range(X):
        for k in range(Z):
            spot = lax.rem(z - k + Z, Z) * X + lax.rem(x - xr + X, X)
            at = pl.ds(pl.multiple_of(spot * rows, 16), rows)
            copies.append(pltpu.make_async_copy(units[xr * Z + k], weights.at[at], sems.at[0]))
    for i in range(tiles):
        copies.append(pltpu.make_async_copy(act_refs[i], acts.at[i], sems.at[0]))
        for s in range(Z):
            at = pl.ds(pl.multiple_of(rows_of(s), own), own)
            copies.append(
                pltpu.make_async_copy(
                    grad_refs[i].at[at], grads.at[i, pl.ds(s * own, own)], sems.at[0]
                )
            )
    for copy in copies:
        copy.start()
    for copy in copies:
        copy.wait()

    def one_tile(i, carry):
        both = dot(acts[i], weights[:, : 2 * n])
        gate, up = both[:, :n], both[:, n:]
        product_grad = dot(grads[i], weights[:, 2 * n :])
        sigma = 1.0 / (1.0 + jnp.exp(-gate))
        silu = gate * sigma
        product = (silu * up).astype(BF16)
        up_grad = (product_grad * silu).astype(BF16)
        gate_grad = (product_grad * up * sigma * (1.0 + gate * (1.0 - sigma))).astype(BF16)
        both_grad = jnp.concatenate([gate_grad, up_grad], 1)
        at = pl.ds(pl.multiple_of(i * tokens, tokens), tokens)
        both_grads[at, :] = both_grad
        in_part = contract_last(both_grad, weights[:, : 2 * n])
        out_part = contract_last(product, weights[:, 2 * n :])
        for s in range(Z):
            spot = pl.ds(pl.multiple_of(i * tokens + rows_of(s), own), own)
            products[spot, :] = product[s * own : (s + 1) * own]

        @pl.when(i == 0)
        def _():
            in_own[...] = in_part
            for s in range(Z):
                spot = pl.ds(pl.multiple_of(rows_of(s), own), own)
                out_own[spot, :] = out_part[s * own : (s + 1) * own]

        @pl.when(i > 0)
        def _():
            low_at = pl.ds(pl.multiple_of((i - 1) * tokens, tokens), tokens)
            in_low[low_at, :] = in_part.astype(BF16)
            for s in range(Z):
                spot = pl.ds(pl.multiple_of((i - 1) * tokens + rows_of(s), own), own)
                out_low[spot, :] = out_part[s * own : (s + 1) * own].astype(BF16)

        return carry

    lax.fori_loop(0, tiles, one_tile, 0)


def hidden_layer(grid, acts, grads, units):
    Z, X, C = grid.Z, grid.X, grid.C
    tokens, width = acts[0].shape
    n = units[0].shape[1] // 3
    shape = jax.ShapeDtypeStruct
    rows = [shape((tokens, width), F32), shape(((C - 1) * tokens, width), BF16)]
    shapes = rows + rows + [shape((C * tokens, 2 * n), BF16), shape((C * tokens, n), BF16)]
    return pl.pallas_call(
        functools.partial(hidden_kernel, Z, X, C, tuple(grid.order)),
        out_shape=shapes,
        in_specs=[pl.BlockSpec(memory_space=pltpu.SMEM)] + [anywhere()] * (2 * C + X * Z),
        out_specs=[whole_vmem()] * len(shapes),
        scratch_shapes=[
            pltpu.VMEM((width, 3 * n), BF16),
            pltpu.VMEM((C, tokens, width), BF16),
            pltpu.VMEM((C, tokens, width), BF16),
            pltpu.SemaphoreType.DMA((1,)),
        ],
        compiler_params=pltpu.CompilerParams(vmem_limit_bytes=36 * 2**20),
        cost_estimate=pl.CostEstimate(
            flops=12 * C * tokens * width * n,
            bytes_accessed=20 * 2**20,
            transcendentals=C * tokens * n,
        ),
    )(grid.where, *acts, *grads, *units)


def norm_kernel(values, more, gain, total, normed):
    hidden = values[...].astype(F32) + more[...].astype(F32)
    recip = lax.rsqrt(jnp.mean(hidden * hidden, -1, keepdims=True) + EPSILON)
    total[...] = hidden
    normed[...] = (hidden * recip * gain[...]).astype(BF16)


def add_norm(values, more, gain):
    return pl.pallas_call(
        norm_kernel,
        out_shape=[
            jax.ShapeDtypeStruct(values.shape, F32),
            jax.ShapeDtypeStruct(values.shape, BF16),
        ],
        in_specs=[whole_vmem()] * 3,
        out_specs=[whole_vmem()] * 2,
        compiler_params=pltpu.CompilerParams(vmem_limit_bytes=32 * 2**20),
    )(values, more, gain)


def norm_back_kernel(number, *refs):
    parts = refs[:number]
    values, beside, gain, grad, low, gain_term = refs[number:]
    part = parts[0][...].astype(F32)
    for ref in parts[1:]:
        part = part + ref[...].astype(F32)
    value = values[...].astype(F32)
    recip = lax.rsqrt(jnp.mean(value * value, -1, keepdims=True) + EPSILON)
    normal = value * recip
    scaled = part * gain[...]
    mean = jnp.mean(scaled * normal, -1, keepdims=True)
    total = beside[...].astype(F32) + recip * (scaled - normal * mean)
    grad[...] = total
    low[...] = total.astype(BF16)
    gain_term[...] = jnp.sum(part * normal, 0, keepdims=True)


def norm_back(parts, values, beside, gain):
    return pl.pallas_call(
        functools.partial(norm_back_kernel, len(parts)),
        out_shape=[
            jax.ShapeDtypeStruct(values.shape, F32),
            jax.ShapeDtypeStruct(values.shape, BF16),
            jax.ShapeDtypeStruct(gain.shape, F32),
        ],
        in_specs=[whole_vmem()] * (3 + len(parts)),
        out_specs=[whole_vmem()] * 3,
        compiler_params=pltpu.CompilerParams(vmem_limit_bytes=32 * 2**20),
    )(*parts, values, beside, gain)


def order_kernel(Z, C, order, where, *refs):
    pieces, out = refs[:-1], refs[-1]
    own = out.shape[0] // (Z * C)
    z, c = where[0], where[3]
    ring = sum(jnp.where(z == value, place, 0) for place, value in enumerate(order))
    for s in range(Z):
        ranked = lax.rem(ring - s + Z, Z)
        at = sum(jnp.where(ranked == place, value, 0) for place, value in enumerate(order))
        for h in range(C):
            spot = pl.multiple_of((at * C + lax.rem(c - h + C, C)) * own, own)
            out[pl.ds(spot, own), :] = pieces[h][s * own : (s + 1) * own, :]


def order_tokens(grid, pieces):
    tokens, width = pieces[0].shape
    return pl.pallas_call(
        functools.partial(order_kernel, grid.Z, grid.C, tuple(grid.order)),
        out_shape=jax.ShapeDtypeStruct((grid.C * tokens, width), BF16),
        in_specs=[pl.BlockSpec(memory_space=pltpu.SMEM)] + [whole_vmem()] * grid.C,
        out_specs=whole_vmem(),
        compiler_params=pltpu.CompilerParams(vmem_limit_bytes=24 * 2**20),
    )(grid.where, *pieces)


def unit_sum_kernel(number, *refs):
    units, outs = refs[:number], refs[number:]
    for k, out in enumerate(outs):
        total = units[0][k].astype(F32)
        for unit in units[1:]:
            total = total + unit[k].astype(F32)
        out[...] = total.astype(BF16)


def unit_sum(units):
    Z, part, n = units[0].shape
    return pl.pallas_call(
        functools.partial(unit_sum_kernel, len(units)),
        out_shape=[jax.ShapeDtypeStruct((part, n), BF16)] * Z,
        in_specs=[whole_vmem()] * len(units),
        out_specs=[whole_vmem()] * Z,
        compiler_params=pltpu.CompilerParams(vmem_limit_bytes=24 * 2**20),
    )(*units)


def sort_kernel(Z, U, Y, where, *refs):
    parts, outs = refs[:Z], refs[Z:]
    z, y = where[0], where[2]
    for k in range(Z):
        source = lax.rem(z - k + Z, Z)
        ahead = lax.rem(lax.div(source, U) - y + Y, Y)
        for r in range(Y):

            @pl.when(ahead == r)
            def _(k=k, r=r, source=source):
                outs[r][lax.rem(source, U)] = parts[k][...]


def sort_heads(grid, parts):
    half, n = parts[0].shape
    return pl.pallas_call(
        functools.partial(sort_kernel, grid.Z, grid.U, grid.Y),
        out_shape=[jax.ShapeDtypeStruct((grid.U, half, n), BF16)] * grid.Y,
        in_specs=[pl.BlockSpec(memory_space=pltpu.SMEM)] + [whole_vmem()] * grid.Z,
        out_specs=[whole_vmem()] * grid.Y,
        compiler_params=pltpu.CompilerParams(vmem_limit_bytes=24 * 2**20),
    )(grid.where, *parts)


def join_kernel(U, Y, sizes, where, *refs):
    parts, outs = refs[:Y], refs[Y:]
    half = parts[0].shape[1]
    for r in range(Y):
        at = pl.multiple_of(lax.rem(where[2] - r + Y, Y) * half, 8)
        for u in range(U):
            first = 0
            for out, size in zip(outs, sizes):
                columns = parts[r][u, :, first : first + size].astype(F32)
                out[pl.ds(at, half), u * size : (u + 1) * size] = columns
                first += size


def join_heads(grid, parts, sizes):
    U, half, _ = parts[0].shape
    return pl.pallas_call(
        functools.partial(join_kernel, U, grid.Y, sizes),
        out_shape=[jax.ShapeDtypeStruct((grid.Y * half, U * size), F32) for size in sizes],
        in_specs=[pl.BlockSpec(memory_space=pltpu.SMEM)] + [whole_vmem()] * grid.Y,
        out_specs=[whole_vmem()] * len(sizes),
        compiler_params=pltpu.CompilerParams(vmem_limit_bytes=24 * 2**20),
    )(grid.where, *parts)


def place_kernel(Y, C, where, *refs):
    parts, out = refs[:-1], refs[-1]
    y, c = where[2], where[3]
    own = parts[0].shape[0]
    for i, part in enumerate(parts):
        at = lax.rem(c - i // Y + C, C) * own
        at = pl.ds(pl.multiple_of(at, own), own)
        out[lax.rem(y - i % Y + Y, Y), at, :] = part[...].astype(F32)


def place_rows(grid, parts):
    own, width = parts[0].shape
    return pl.pallas_call(
        functools.partial(place_kernel, grid.Y, grid.C),
        out_shape=jax.ShapeDtypeStruct((grid.Y, grid.C * own, width), F32),
        in_specs=[pl.BlockSpec(memory_space=pltpu.SMEM)] + [whole_vmem()] * len(parts),
        out_specs=whole_vmem(),
        compiler_params=pltpu.CompilerParams(vmem_limit_bytes=32 * 2**20),
    )(grid.where, *parts)


def core_sum_kernel(number, own, *refs):
    lows, outs = refs[:number], refs[number:]
    total = own[...]
    for low in lows:
        total = total + low[...].astype(F32)
    if len(outs) == 1:
        outs[0][...] = total.astype(outs[0].dtype)
        return
    half = total.shape[0] // 2
    outs[0][...] = total[:half].astype(outs[0].dtype)
    outs[1][...] = total[half:].astype(outs[1].dtype)


def core_sum(own, lows, kind, pieces):
    rows, width = own.shape
    return pl.pallas_call(
        functools.partial(core_sum_kernel, len(lows)),
        out_shape=[jax.ShapeDtypeStruct((rows // pieces, width), kind)] * pieces,
        in_specs=[whole_vmem()] * (1 + len(lows)),
        out_specs=[whole_vmem()] * pieces,
        compiler_params=pltpu.CompilerParams(vmem_limit_bytes=32 * 2**20),
    )(own, *lows)


def hidden_weight_kernel(X, tiles, where, *refs):
    take = Taker(refs)
    acts, grads = take(tiles), take(tiles)
    Y = (len(refs) - 2 * tiles - X - 1) // 2
    both_grads, products, outs, total = take(Y), take(Y), take(X), take(1)[0]
    x = where[1]
    tokens = acts[0].shape[0]
    rows = outs[0].shape[0]
    n = products[0].shape[1]

    def summed(parts, values):
        sums = None
        for i in range(tiles):
            at = i // Y * tokens
            part = contract_first(parts[i][...], values[i % Y][at : at + tokens, :])
            sums = part if sums is None else sums + part
        return sums

    total[:, : 2 * n] = summed(acts, both_grads)
    total[:, 2 * n :] = summed(grads, products)
    for xr in range(X):
        at = pl.ds(pl.multiple_of(lax.rem(x + xr, X) * rows, 8), rows)
        outs[xr][...] = total[at, :].astype(BF16)


def hidden_weight_grad(grid, k, acts, grads, both_grads, products):
    Z, X, tiles = grid.Z, grid.X, len(acts)
    tokens, width = acts[0].shape
    n = products[0].shape[1]
    block = width // Z

    def features(i, s):
        return (0, lax.rem(s[0] + k, Z))

    return pl.pallas_call(
        functools.partial(hidden_weight_kernel, X, tiles),
        out_shape=[jax.ShapeDtypeStruct((block // X, 3 * n), BF16)] * X,
        grid_spec=pltpu.PrefetchScalarGridSpec(
            num_scalar_prefetch=1,
            grid=(1,),
            in_specs=[pl.BlockSpec((tokens, block), features)] * (2 * tiles)
            + [pl.BlockSpec(value.shape, lambda i, s: (0, 0)) for value in both_grads + products],
            out_specs=[pl.BlockSpec((block // X, 3 * n), lambda i, s: (0, 0))] * X,
            scratch_shapes=[pltpu.VMEM((block, 3 * n), F32)],
        ),
        compiler_params=pltpu.CompilerParams(vmem_limit_bytes=26 * 2**20),
        cost_estimate=pl.CostEstimate(
            flops=6 * tiles * tokens * block * n, bytes_accessed=10 * 2**20, transcendentals=0
        ),
    )(grid.where, *acts, *grads, *both_grads, *products)


def weight_kernel(X, Y, where, act, grad, *refs):
    outs, total = refs[: Y * X], refs[Y * X]
    x, y = where[1], where[2]
    part = outs[0].shape[1]
    total[...] = contract_first(act[...], grad[...])
    for xr in range(X):
        for yr in range(Y):
            at = (lax.rem(x + xr, X) * Y + lax.rem(y + yr, Y)) * part
            at = pl.ds(pl.multiple_of(at, 8), part)
            outs[yr * X + xr][0] = total[at, :].astype(BF16)


def weight_grad(grid, act, grad):
    Z, X, Y = grid.Z, grid.X, grid.Y
    tokens, width = act.shape
    n = grad.shape[1]
    part = width // (Z * X * Y)
    return pl.pallas_call(
        functools.partial(weight_kernel, X, Y),
        out_shape=[jax.ShapeDtypeStruct((Z, part, n), BF16)] * (Y * X),
        grid_spec=pltpu.PrefetchScalarGridSpec(
            num_scalar_prefetch=1,
            grid=(Z,),
            in_specs=[
                pl.BlockSpec((tokens, width // Z), lambda k, s: (0, lax.rem(s[0] + k, Z))),
                pl.BlockSpec((tokens, n), lambda k, s: (0, 0)),
            ],
            out_specs=[pl.BlockSpec((1, part, n), lambda k, s: (k, 0, 0))] * (Y * X),
            scratch_shapes=[pltpu.VMEM((width // Z, n), F32)],
        ),
        compiler_params=pltpu.CompilerParams(vmem_limit_bytes=26 * 2**20),
        cost_estimate=pl.CostEstimate(
            flops=2 * tokens * width * n, bytes_accessed=2 * width * n, transcendentals=0
        ),
    )(grid.where, act, grad)


def identity(number):
    row = lax.broadcasted_iota(jnp.int32, (number, number), 0)
    column = lax.broadcasted_iota(jnp.int32, (number, number), 1)
    return jnp.where(row == column, 1.0, 0.0).astype(BF16)


def visible(X, rows, where, limit, first, tile, keys):
    x = where[1]
    key = lax.broadcasted_iota(jnp.int32, (keys, 1), 0)
    tokens = keys // X
    inside = lax.rem(key, tokens)
    key_x = lax.rem(x - lax.div(key, tokens) + X, X)
    key_pos = (lax.div(inside, rows) * X + key_x) * rows + lax.rem(inside, rows)
    query = first + lax.broadcasted_iota(jnp.int32, (1, tile), 1)
    query_pos = (lax.div(query, rows) * X + x) * rows + lax.rem(query, rows)
    return (key_pos <= query_pos) | (key_pos < limit)


def split_heads(qkv, others, queries, keys_values, turned, group):
    tokens = qkv.shape[0]
    for g in range(group):
        queries[g] = qkv[:, g * HEAD_DIM : (g + 1) * HEAD_DIM]
    eye = identity(2 * HEAD_DIM)
    for i in range(1 + len(others)):
        at = slice(i * tokens, (i + 1) * tokens)
        both = qkv[:, group * HEAD_DIM : (group + 2) * HEAD_DIM] if i == 0 else others[i - 1][...]
        keys_values[0, at, :] = both[:, :HEAD_DIM]
        keys_values[1, at, :] = both[:, HEAD_DIM:]
        turned[:, at] = contract_last(eye, both).astype(BF16)


def attend_kernel(X, rows, group, tile, where, prefix, qkv, *refs):
    take = Taker(refs)
    others, heads, stats = take(X - 1), take(1)[0], take(1)[0]
    queries, keys_values, turned = take(3)
    tokens = qkv.shape[0]
    scale = HEAD_DIM ** (-0.5)
    split_heads(qkv, others, queries, keys_values, turned, group)
    limit = prefix[where[2]]
    for t in range(tokens // tile):
        at = slice(t * tile, (t + 1) * tile)
        allowed = visible(X, rows, where, limit, t * tile, tile, X * tokens)
        outs = []
        for g in range(group):
            scores = contract_last(keys_values[0], queries[g, at, :]) * scale
            scores = jnp.where(allowed, scores, NEGATIVE)
            top = jnp.max(scores, 0, keepdims=True)
            expo = jnp.exp(scores - top)
            total = jnp.sum(expo, 0, keepdims=True)
            probs = (expo / total).astype(BF16)
            outs.append(jnp.transpose(dot(turned[HEAD_DIM:, :], probs)).astype(BF16))
            stats[g : g + 1, at] = top
            stats[group + g : group + g + 1, at] = total
        heads[at, :] = jnp.concatenate(outs, 1)


def attend_back_kernel(X, rows, group, tile, where, prefix, qkv, *refs):
    take = Taker(refs)
    others, heads_grad, stats = take(X - 1), take(1)[0], take(1)[0]
    query_grad, kv_grads = take(1)[0], take(X)
    queries, keys_values, turned, grads, key_sum, value_sum = take(6)
    tokens = qkv.shape[0]
    scale = HEAD_DIM ** (-0.5)
    split_heads(qkv, others, queries, keys_values, turned, group)
    for g in range(group):
        grads[g] = heads_grad[:, g * HEAD_DIM : (g + 1) * HEAD_DIM]
    limit = prefix[where[2]]
    for t in range(tokens // tile):
        at = slice(t * tile, (t + 1) * tile)
        allowed = visible(X, rows, where, limit, t * tile, tile, X * tokens)
        outs = []
        for g in range(group):
            query, grad = queries[g, at, :], grads[g, at, :]
            scores = contract_last(keys_values[0], query) * scale
            scores = jnp.where(allowed, scores, NEGATIVE)
            probs = jnp.exp(scores - stats[g : g + 1, at]) / stats[group + g : group + g + 1, at]
            prob_grad = contract_last(keys_values[1], grad)
            mean = jnp.sum(probs * prob_grad, 0, keepdims=True)
            score_grad = (probs * (prob_grad - mean)).astype(BF16)
            out = jnp.transpose(dot(turned[:HEAD_DIM, :], score_grad)) * scale
            outs.append(out.astype(BF16))
            key_part = dot(score_grad, query)
            value_part = dot(probs.astype(BF16), grad)
            if t == 0 and g == 0:
                key_sum[...] = key_part
                value_sum[...] = value_part
            else:
                key_sum[...] += key_part
                value_sum[...] += value_part
        query_grad[at, :] = jnp.concatenate(outs, 1)
    for i, out in enumerate(kv_grads):
        at = slice(i * tokens, (i + 1) * tokens)
        out[:, :HEAD_DIM] = (key_sum[at, :] * scale).astype(out.dtype)
        out[:, HEAD_DIM:] = value_sum[at, :].astype(out.dtype)


def query_tile(tokens, keys):
    tile = tokens
    while tile > 128 and tile * keys > 2**19:
        tile = tile // 2
    return tile


def attend(grid, rows, group, prefix, qkv, others):
    tokens, keys = qkv.shape[0], grid.X * qkv.shape[0]
    smem = pl.BlockSpec(memory_space=pltpu.SMEM)
    return pl.pallas_call(
        functools.partial(attend_kernel, grid.X, rows, group, query_tile(tokens, keys)),
        out_shape=[
            jax.ShapeDtypeStruct((tokens, group * HEAD_DIM), BF16),
            jax.ShapeDtypeStruct((2 * group, tokens), F32),
        ],
        in_specs=[smem, smem] + [whole_vmem()] * grid.X,
        out_specs=[whole_vmem()] * 2,
        scratch_shapes=[
            pltpu.VMEM((group, tokens, HEAD_DIM), BF16),
            pltpu.VMEM((2, keys, HEAD_DIM), BF16),
            pltpu.VMEM((2 * HEAD_DIM, keys), BF16),
        ],
        compiler_params=pltpu.CompilerParams(vmem_limit_bytes=36 * 2**20),
        cost_estimate=pl.CostEstimate(
            flops=8 * group * tokens * keys * 128,
            bytes_accessed=4 * 2**20,
            transcendentals=group * tokens * keys,
        ),
    )(grid.where, prefix, qkv, *others)


def attend_back(grid, rows, group, prefix, qkv, others, heads_grad, stats):
    tokens, keys = qkv.shape[0], grid.X * qkv.shape[0]
    smem = pl.BlockSpec(memory_space=pltpu.SMEM)
    return pl.pallas_call(
        functools.partial(attend_back_kernel, grid.X, rows, group, query_tile(tokens, keys)),
        out_shape=[jax.ShapeDtypeStruct((tokens, group * HEAD_DIM), BF16)]
        + [jax.ShapeDtypeStruct((tokens, 2 * HEAD_DIM), F32)]
        + [jax.ShapeDtypeStruct((tokens, 2 * HEAD_DIM), BF16)] * (grid.X - 1),
        in_specs=[smem, smem] + [whole_vmem()] * (grid.X + 2),
        out_specs=[whole_vmem()] * (1 + grid.X),
        scratch_shapes=[
            pltpu.VMEM((group, tokens, HEAD_DIM), BF16),
            pltpu.VMEM((2, keys, HEAD_DIM), BF16),
            pltpu.VMEM((2 * HEAD_DIM, keys), BF16),
            pltpu.VMEM((group, tokens, HEAD_DIM), BF16),
            pltpu.VMEM((keys, HEAD_DIM), F32),
            pltpu.VMEM((keys, HEAD_DIM), F32),
        ],
        compiler_params=pltpu.CompilerParams(vmem_limit_bytes=36 * 2**20),
        cost_estimate=pl.CostEstimate(
            flops=16 * group * tokens * keys * 128,
            bytes_accessed=4 * 2**20,
            transcendentals=group * tokens * keys,
        ),
    )(grid.where, prefix, qkv, *others, heads_grad, stats)


class Grid:
    def __init__(self, dp, tensor, seqs, kv_local):
        self.Y = seqs
        self.C = tensor // seqs
        self.U = kv_local
        self.Z = seqs * kv_local
        self.X = dp // self.Z
        assert self.C * self.Y == tensor and self.X * self.Z == dp
        i, j = lax.axis_index("dp"), lax.axis_index("tensor")
        self.z, self.x = i // self.X, i % self.X
        self.y, self.c = j // self.C, j % self.C
        self.where = jnp.stack([self.z, self.x, self.y, self.c]).astype(jnp.int32)
        order = list(range(0, self.Z, 2)) + list(range(1, self.Z, 2))[::-1]
        self.order = order
        self.ring = [order.index(z) for z in range(self.Z)]

    def move(self, value, target):
        pairs = []
        for z in range(self.Z):
            for x in range(self.X):
                for y in range(self.Y):
                    for c in range(self.C):
                        tz, tx, ty, tc = target(z, x, y, c)
                        here = ((z * self.X + x) * self.Y + y) * self.C + c
                        there = ((tz * self.X + tx) * self.Y + ty) * self.C + tc
                        pairs.append((here, there))
        return lax.ppermute(value, AXES, pairs)

    def to_z(self, value, k):
        return self.move(value, lambda z, x, y, c: ((z + k) % self.Z, x, y, c))

    def hop_z(self, value, k):
        if 1 < k < self.Z - 1:
            return self.to_z(self.to_z(value, 1), k - 1)
        return self.to_z(value, k)

    def to_x(self, value, k):
        return self.move(value, lambda z, x, y, c: (z, (x + k) % self.X, y, c))

    def to_y(self, value, k):
        return self.move(value, lambda z, x, y, c: (z, x, (y + k) % self.Y, c))

    def to_c(self, value, k):
        return self.move(value, lambda z, x, y, c: (z, x, y, (c + k) % self.C))

    def along_ring(self, value, k):
        return self.move(
            value, lambda z, x, y, c: (self.order[(self.ring[z] + k) % self.Z], x, y, c)
        )

    def slot_z(self, s):
        place_of = sum(jnp.where(self.z == z, ring, 0) for z, ring in enumerate(self.ring))
        place_of = (place_of - s) % self.Z
        return sum(jnp.where(place_of == at, z, 0) for at, z in enumerate(self.order))

    def to_xy(self, value, kx, ky):
        return self.move(
            value, lambda z, x, y, c: (z, (x + kx) % self.X, (y + ky) % self.Y, c)
        )

    def groups(self, names):
        sizes = {"z": self.Z, "x": self.X, "y": self.Y, "c": self.C}
        members = {}
        for z in range(self.Z):
            for x in range(self.X):
                for y in range(self.Y):
                    for c in range(self.C):
                        at = {"z": z, "x": x, "y": y, "c": c}
                        key = tuple(at[name] for name in sizes if name not in names)
                        rank = 0
                        for name in names:
                            rank = rank * sizes[name] + at[name]
                        index = ((z * self.X + x) * self.Y + y) * self.C + c
                        members.setdefault(key, {})[rank] = index
        return [[group[rank] for rank in range(len(group))] for group in members.values()]

    def gather(self, own, names):
        return lax.all_gather(own, AXES, axis=0, tiled=True, axis_index_groups=self.groups(names))

    def scatter(self, partial, names):
        return lax.psum_scatter(
            partial,
            AXES,
            scatter_dimension=0,
            tiled=True,
            axis_index_groups=self.groups(names),
        )

    def ring_steps(self, own, steps):
        blocks = [own]
        for _ in range(steps):
            blocks.append(self.along_ring(blocks[-1], 1))
        return blocks

    def spread_yc(self, mine):
        pieces = [mine] + [self.to_y(mine, k) for k in range(1, self.Y)]
        return pieces + [self.to_c(piece, k) for k in range(1, self.C) for piece in pieces]

    def gather_wide(self, blocks, hold=()):
        half = self.Z // 2
        first = jnp.concatenate(blocks[:half], 0)
        second = jnp.concatenate(blocks[half:], 0)
        pieces = [jnp.concatenate([first, second], 0)]
        for k in range(1, self.Y):
            pieces.append(
                jnp.concatenate([after(self.to_y(first, k), *hold), self.to_y(second, k)], 0)
            )
        return pieces + [self.to_c(piece, k) for k in range(1, self.C) for piece in pieces]

    def ring_sum(self, slots, holds=()):
        total = slots[-1].astype(BF16)
        for i, s in enumerate(range(self.Z - 2, -1, -1)):
            if i < len(holds):
                total = after(total, *holds[i])
            arrived = self.along_ring(total, -1)
            total = arrived.astype(F32) + slots[s]
            if s > 0:
                total = total.astype(BF16)
        return arrived, slots[0]

    def exchange_z(self, parts):
        return [parts[0]] + [self.to_z(parts[k], k) for k in range(1, self.Z)]

    def spread_xy(self, unit):
        return [
            unit if xr == yr == 0 else self.to_xy(unit, xr, yr)
            for yr in range(self.Y)
            for xr in range(self.X)
        ]

    def send_xy(self, units):
        return [
            unit if i == 0 else self.to_xy(unit, i % self.X, i // self.X)
            for i, unit in enumerate(units)
        ]

    def return_heads(self, parts, sizes):
        sorted_parts = sort_heads(self, parts)
        arrived = [sorted_parts[0]] + [self.to_y(sorted_parts[r], r) for r in range(1, self.Y)]
        return join_heads(self, arrived, sizes)

    def from_z(self, k):
        return (self.z - k) % self.Z

    def spread_x(self, unit):
        parts = [unit] + [self.to_x(unit, k) for k in range(1, self.X)]
        return place(parts, [(self.x - k) % self.X for k in range(self.X)])

    def gather_gains(self, gains):
        xs = self.spread_x(gains)
        parts = [xs] + [self.to_z(xs, k) for k in range(1, self.Z)]
        whole = place(parts, [self.from_z(k) for k in range(self.Z)])
        return whole.transpose(2, 0, 1, 3).reshape(gains.shape[0], -1)

    def sum_gains(self, terms, hold):
        number = terms.shape[0]
        part = terms
        for k in range(1, self.C):
            part = part + self.to_c(terms, k)
        terms = part
        for k in range(1, self.Y):
            part = part + self.to_y(terms, k)
        part = after(part, *hold)
        part = part.reshape(number, self.Z, self.X, -1).transpose(2, 1, 0, 3)
        out = pick(part, self.x)
        for k in range(1, self.X):
            out = out + self.to_x(pick(part, (self.x + k) % self.X), k)
        return sum(self.exchange_z([pick(out, (self.z + k) % self.Z) for k in range(self.Z)]))


def per_device(
    dp,
    tensor,
    inputs,
    cotangent,
    prefix,
    gain_attn,
    w_query,
    w_key,
    w_value,
    w_out,
    gain_mlp,
    w_gate,
    w_up,
    w_down,
):
    seqs, rows, width = inputs.shape
    kv_local = w_key.shape[1] // HEAD_DIM
    group = w_query.shape[1] // w_key.shape[1]
    grid = Grid(dp, tensor, seqs, kv_local)
    own = rows // grid.C
    q_cols = group * HEAD_DIM

    def own_rows(value):
        return lax.dynamic_slice(value, (grid.y, grid.c * own, 0), (1, own, width))[0]

    others = range(1, grid.X)
    middle = grid.Z // 2
    ends = [k for k in range(1, grid.Z) if k != middle]
    cot_own = own_rows(cotangent)
    cot_all = grid.gather(cot_own, "z")
    near = pack_heads(grid, [after(w_query, cot_own), w_key, w_value])
    near_own = near[0]
    near = [near_own] + [grid.to_y(near[k], k) for k in range(1, grid.Y)]
    gains = grid.gather_gains(jnp.stack([after(gain_attn, cot_own), gain_mlp], 0))
    flat = own_rows(inputs)
    gain_one, gain_two = gains[0:1].astype(F32), gains[1:2].astype(F32)
    values = flat.astype(F32)
    recip = lax.rsqrt(jnp.mean(values * values, -1, keepdims=True) + EPSILON)
    attn_own = after((values * recip * gain_one).astype(BF16), *near)
    qkv_parts = grid.exchange_z(route_heads(grid, near))

    packed = pack_hidden(grid, after(w_gate, attn_own), w_up, w_down.T)
    out_near = pack_heads(grid, [after(w_out.T, packed[0])])
    out_near = [out_near[0]] + [grid.to_y(out_near[k], k) for k in range(1, grid.Y)]

    def ring_on(blocks, *hold):
        return blocks + [grid.along_ring(after(blocks[-1], *hold), 1)]

    blocks = ring_on([attn_own])
    blocks = ring_on(blocks, *packed[:1])
    blocks = ring_on(blocks, *qkv_parts, *[cot_all])
    for _ in range(grid.Z - 4):
        blocks = ring_on(blocks)
    qkv_units = grid.spread_xy(jnp.stack(qkv_parts, 0))
    out_parts = route_heads(grid, [after(part, *qkv_parts) for part in out_near])
    out_parts = grid.exchange_z(out_parts)
    mine = after(jnp.concatenate(blocks, 0), *qkv_units[1:], *out_parts[1:])
    attn_in = order_tokens(grid, [mine] + [grid.to_c(mine, k) for k in range(1, grid.C)])

    w_qkv = assemble(grid, qkv_units)
    w_qkv = w_qkv[:, : q_cols + 2 * HEAD_DIM]
    qkv = dot(attn_in, w_qkv).astype(BF16)
    tokens = qkv.shape[0]
    kv_own = qkv[:, q_cols:]
    kv_others = [grid.to_x(kv_own, k) for k in others]
    out_units = grid.spread_xy(after(jnp.stack(out_parts, 0), *qkv_units[1:]))
    w_o = assemble(grid, out_units)[:, :q_cols]
    arrived, first, hop = {0: packed[0]}, out_parts[1:], []
    for k in [middle] + ends:
        part = after(packed[k], *first)
        if k == middle and middle > 1:
            hop = [grid.to_z(part, 1)]
            arrived[k] = grid.to_z(after(hop[0], *out_units[1:]), middle - 1)
        else:
            arrived[k] = grid.to_z(part, k)
        first = [arrived[k]]
    ready = after(qkv, *out_units[1:], *hop)
    heads, stats = attend(grid, rows, group, prefix, ready, kv_others)
    moved_x, first = {}, out_units[1:]
    for k in [0, middle] + ends:
        moved_x[k] = [grid.to_x(after(arrived[k], *first), x) for x in others]
        first = moved_x[k]
    mlp_grad = grid.spread_yc(after(cot_all, *out_units[1:]))
    attn_partial = contract_last(after(heads, *[arrived[middle]]), w_o).astype(BF16)
    attn_out = grid.scatter(attn_partial, "zc")
    held = list(mlp_grad[: grid.Y]) + list([arrived[ends[0]]]) + list(moved_x[middle])
    hidden, mlp_own = add_norm(flat, after(attn_out, *held), gain_two)
    mlp_blocks = ring_on([mlp_own])
    mlp_blocks = ring_on(mlp_blocks)
    for _ in range(grid.Z - 3):
        mlp_blocks = ring_on(mlp_blocks, *[arrived[ends[-1]]])
    mlp_in = grid.gather_wide(mlp_blocks, list(moved_x[ends[-1]]))
    units = [arrived[k] for k in range(grid.Z)]
    units = units + [moved_x[k][x - 1] for x in others for k in range(grid.Z)]

    layers, in_moved, hold = [None] * grid.Y, [], ()
    for yr in range(grid.Y - 1, -1, -1):
        acts = [mlp_in[c * grid.Y + yr] for c in range(grid.C)]
        acts[0] = after(acts[0], *hold)
        grads = [mlp_grad[c * grid.Y + yr] for c in range(grid.C)]
        layers[yr] = hidden_layer(grid, acts, grads, units)
        each = acts[0].shape[0]
        half = each // 2
        low = after(layers[yr][1], *[sent[0] for sent in in_moved])
        moved = [grid.to_c(low[(h - 1) * each : h * each], -h) for h in range(1, grid.C)]
        if yr > 0:
            hold = core_sum(layers[yr][0], moved, BF16, 2)
            in_moved.append([grid.to_y(hold[1], -yr), grid.to_y(hold[0], -yr)])
    both_grads = [layer[4] for layer in layers]
    products = [layer[5] for layer in layers]

    order = [middle] + ends + [0]
    swapped, hidden_parts, holds = [], [None] * grid.Z, []
    for at, k in enumerate(order):
        hold = [in_late] if at else []
        given = both_grads[:-1] + [after(both_grads[-1], *hold)]
        parts = list(hidden_weight_grad(grid, k, mlp_in, mlp_grad, given, products))
        if at == 0:
            in_late, in_first = core_sum(after(layers[0][0], *parts), moved, F32, 2)
        first = swapped[-1] if swapped else []
        swapped.append([grid.to_x(after(parts[xr], *first), xr) for xr in others])
        holds.append(parts)
    for at, k in enumerate(order):
        late = list(holds[1]) + list(holds[2]) if at == 0 else []
        hidden_parts[k] = core_sum(after(holds[at][0], *late), swapped[at], BF16, 1)[0]
    for sent in in_moved:
        in_first = in_first + sent[0].astype(F32)
    in_late = after(in_late, in_first)
    for sent in in_moved:
        in_late = in_late + sent[1].astype(F32)
    slots = [
        (in_late, in_first)[2 * s // grid.Z][s % (grid.Z // 2) * own :][:own]
        for s in range(grid.Z)
    ]
    last = holds[3]
    holds = [
        [],
        list(holds[1]),
        list(holds[2]) + list([hidden_parts[middle]]),
    ]
    in_parts = grid.ring_sum(slots, holds)
    arrived, first, hop = list(hidden_parts), [], None
    for k in order[:-1]:
        part = after(hidden_parts[k], *first)
        if k == middle and middle > 1:
            hop = grid.to_z(part, 1)
            arrived[k] = grid.to_z(hop, middle - 1)
        else:
            arrived[k] = grid.to_z(part, k)
        first = [arrived[k]]
    held = list(swapped[1]) + list(swapped[2]) + list([arrived[middle]])
    held = held
    in_parts = (after(in_parts[0], *held), in_parts[1])
    hidden_grad, hidden_low, gain_two_term = norm_back(in_parts, hidden, cot_own, gain_two)
    out_y, out_sent, moved_out = [], [], [None] * grid.Y
    for yr in range(grid.Y - 1, -1, -1):
        low = after(layers[yr][3], in_parts[0])
        moved_out[yr] = [grid.to_c(low[(h - 1) * each : h * each], -h) for h in range(1, grid.C)]
        if yr > 0:
            out_sent.append(core_sum(layers[yr][2], moved_out[yr], BF16, 1)[0])
            out_y.append(grid.to_y(out_sent[-1], -yr))
    blocks = ring_on([hidden_low])
    blocks = ring_on(blocks, *out_sent, *moved_out[0])
    for _ in range(grid.Z - 3):
        held = list(last) + list(swapped[3])
        held = held
        blocks = ring_on(blocks, *held)
    mine = jnp.concatenate(blocks, 0)
    pieces = [mine] + [grid.to_c(mine, k) for k in range(1, grid.C)]
    held = []
    pieces[-1] = after(pieces[-1], *held)
    attn_grad = order_tokens(grid, pieces)
    out_sum = core_sum(layers[0][2], moved_out[0] + out_y, BF16, 1)[0]
    mlp_out = grid.scatter(after(out_sum, *[attn_grad]), "z")
    heads_grad = dot(attn_grad, w_o).astype(BF16)
    out_units = weight_grad(grid, attn_grad, heads)

    held = list(out_units) + [out_sum]
    heads_grad = after(heads_grad, *held)
    query_grad, *kv_parts = attend_back(
        grid, rows, group, prefix, qkv, kv_others, heads_grad, stats
    )
    kv_moved = [grid.to_x(kv_parts[k], -k) for k in others]
    out_moved = grid.send_xy(out_units)
    held = list(out_moved[1:]) + list([arrived[order[2]]])
    held = held
    kv_grad = after(kv_parts[0], *held)
    for part in kv_moved:
        kv_grad = kv_grad + part.astype(F32)
    qkv_grad = jnp.concatenate(
        [query_grad, kv_grad.astype(BF16)], 1
    )

    def spread_y(value):
        return [value] + [grid.to_y(value, k) for k in range(1, grid.Y)]

    def spread_c(ys):
        cs = [grid.to_c(part, k) for k in range(1, grid.C) for part in ys]
        return place_rows(grid, ys + cs)

    qkv_units = weight_grad(grid, attn_in, qkv_grad)
    qkv_moved = grid.send_xy(qkv_units)
    out_sums = unit_sum([after(unit) for unit in out_moved])
    out_parts = grid.exchange_z(out_sums)
    held = list(qkv_units) + list(out_parts[1:]) + list([arrived[order[2]]])
    held = held
    partial = contract_last(after(qkv_grad, *held), w_qkv).astype(BF16)
    attn_in_grad = grid.scatter(partial, "zc")
    gate_wgrad, up_wgrad, down_wgrad = unpack_hidden(
        grid, [after(part, *[partial]) for part in arrived]
    )
    out_wgrad = grid.return_heads(out_parts, (q_cols,))[0]
    result_low = (hidden + after(mlp_out, *[partial]).astype(F32)).astype(BF16)
    result = spread_c(spread_y(result_low))
    held = [gate_wgrad]
    held = held
    qkv_sums = unit_sum([after(unit, *held) for unit in qkv_moved])
    qkv_parts = grid.exchange_z(qkv_sums)
    qkv_wgrad = grid.return_heads(qkv_parts, (q_cols, HEAD_DIM, HEAD_DIM))
    held = list(qkv_sums) + [out_wgrad] + list(qkv_wgrad)
    held = held
    ready = after(attn_in_grad, *held)
    _, input_low, gain_one_term = norm_back([ready], flat, hidden_grad, gain_one)
    input_ys = spread_y(input_low)
    input_grad = spread_c(input_ys)
    gain_sum = grid.sum_gains(
        jnp.concatenate([gain_one_term, gain_two_term], 0),
        [],
    )
    down_wgrad = down_wgrad.T

    return (
        result,
        input_grad,
        gain_sum[0],
        qkv_wgrad[0],
        qkv_wgrad[1],
        qkv_wgrad[2],
        out_wgrad.T,
        gain_sum[1],
        gate_wgrad,
        up_wgrad,
        down_wgrad,
    )


def solution(mesh):
    dp, tensor = mesh.shape["dp"], mesh.shape["tensor"]

    def step(*args):
        return per_device(dp, tensor, *args)

    return jax.shard_map(
        step,
        mesh=mesh,
        in_specs=(
            P(None, "dp", None),
            P(None, "dp", None),
            P(),
            P("dp"),
            P("dp", "tensor"),
            P("dp", "tensor"),
            P("dp", "tensor"),
            P("tensor", "dp"),
            P("dp"),
            P("dp", "tensor"),
            P("dp", "tensor"),
            P("tensor", "dp"),
        ),
        out_specs=(
            P(None, "dp", None),
            P(None, "dp", None),
            P("dp"),
            P("dp", "tensor"),
            P("dp", "tensor"),
            P("dp", "tensor"),
            P("tensor", "dp"),
            P("dp"),
            P("dp", "tensor"),
            P("dp", "tensor"),
            P("tensor", "dp"),
        ),
        check_vma=False,
    )
```

```python
import functools

import jax
import jax.numpy as jnp
from jax import lax
from jax.experimental import pallas as pl
from jax.experimental.pallas import tpu as pltpu
from jax.sharding import PartitionSpec as P

HEAD_DIM = 80
EPSILON = 1e-05
NEGATIVE = -1e30
BF16 = jnp.bfloat16
F32 = jnp.float32
AXES = ("dp", "tensor")


def dot(left, right):
    return jnp.dot(left, right, preferred_element_type=F32)


def contract_last(left, right):
    return lax.dot_general(left, right, (((1,), (1,)), ((), ())), preferred_element_type=F32)


def contract_first(left, right):
    return lax.dot_general(left, right, (((0,), (0,)), ((), ())), preferred_element_type=F32)


def after(value, *others):
    return lax.optimization_barrier((value,) + others)[0]


def pick(stack, index):
    return lax.dynamic_index_in_dim(stack, index, 0, keepdims=False)


def place(parts, indices):
    total = jnp.zeros((len(parts),) + parts[0].shape, parts[0].dtype)
    for part, index in zip(parts, indices):
        total = lax.dynamic_update_index_in_dim(total, part, index, 0)
    return total


def whole_vmem():
    return pl.BlockSpec(memory_space=pltpu.VMEM)


def anywhere():
    return pl.BlockSpec(memory_space=pl.ANY)


class Taker:
    def __init__(self, refs):
        self.refs, self.at = refs, 0

    def __call__(self, number):
        taken = self.refs[self.at : self.at + number]
        self.at += number
        return taken


def pack_kernel(Z, where, gate, up, down, *outs):
    n = gate.shape[1] // Z
    for k in range(Z):
        wanted = lax.rem(where[0] + k, Z)
        for s in range(Z):

            @pl.when(wanted == s)
            def _(k=k, s=s):
                for i, weight in enumerate((gate, up, down)):
                    outs[k][:, i * n : (i + 1) * n] = weight[:, s * n : (s + 1) * n]


def pack_hidden(grid, w_gate, w_up, w_down_t):
    rows, cols = w_gate.shape
    return pl.pallas_call(
        functools.partial(pack_kernel, grid.Z),
        out_shape=[jax.ShapeDtypeStruct((rows, 3 * cols // grid.Z), BF16)] * grid.Z,
        in_specs=[pl.BlockSpec(memory_space=pltpu.SMEM)] + [whole_vmem()] * 3,
        out_specs=[whole_vmem()] * grid.Z,
        compiler_params=pltpu.CompilerParams(vmem_limit_bytes=32 * 2**20),
    )(grid.where, w_gate, w_up, w_down_t)


def unpack_kernel(Z, where, *refs):
    parts, outs = refs[:Z], refs[Z:]
    n = parts[0].shape[1] // 3
    for k in range(Z):
        block = lax.rem(where[0] - k + Z, Z)
        for s in range(Z):

            @pl.when(block == s)
            def _(k=k, s=s):
                for i in range(3):
                    outs[i][:, s * n : (s + 1) * n] = parts[k][:, i * n : (i + 1) * n].astype(F32)


def unpack_hidden(grid, parts):
    rows, n = parts[0].shape
    return pl.pallas_call(
        functools.partial(unpack_kernel, grid.Z),
        out_shape=[jax.ShapeDtypeStruct((rows, grid.Z * n // 3), F32)] * 3,
        in_specs=[pl.BlockSpec(memory_space=pltpu.SMEM)] + [whole_vmem()] * grid.Z,
        out_specs=[whole_vmem()] * 3,
        compiler_params=pltpu.CompilerParams(vmem_limit_bytes=32 * 2**20),
    )(grid.where, *parts)


def pack_heads_kernel(U, Y, sizes, where, *refs):
    take = Taker(refs)
    sources, outs, weights, sems = take(len(sizes)), take(Y), take(len(sizes)), take(1)[0]
    copies = [
        pltpu.make_async_copy(source, weight, sems.at[i])
        for i, (source, weight) in enumerate(zip(sources, weights))
    ]
    for copy in copies:
        copy.start()
    for copy in copies:
        copy.wait()
    half = outs[0].shape[1]
    y = where[2]
    for u in range(U):
        first = 0
        for weight, size in zip(weights, sizes):
            columns = weight[:, u * size : (u + 1) * size].astype(F32)
            for k in range(Y):
                part = columns[:half]
                for h in range(1, Y):
                    chosen = lax.rem(y + k, Y) == h
                    part = jnp.where(chosen, columns[h * half : (h + 1) * half], part)
                outs[k][u, :, first : first + size] = part.astype(BF16)
            first += size
        spare = outs[0].shape[2] - first
        if spare:
            for k in range(Y):
                outs[k][u, :, first:] = jnp.zeros((half, spare), BF16)


def pack_heads(grid, weights):
    U, Y = grid.U, grid.Y
    rows = weights[0].shape[0]
    sizes = tuple(weight.shape[1] // U for weight in weights)
    n = -(-sum(sizes) // 128) * 128
    return pl.pallas_call(
        functools.partial(pack_heads_kernel, U, Y, sizes),
        out_shape=[jax.ShapeDtypeStruct((U, rows // Y, n), BF16)] * Y,
        in_specs=[pl.BlockSpec(memory_space=pltpu.SMEM)] + [anywhere()] * len(weights),
        out_specs=[whole_vmem()] * Y,
        scratch_shapes=[pltpu.VMEM(weight.shape, BF16) for weight in weights]
        + [pltpu.SemaphoreType.DMA((len(weights),))],
        compiler_params=pltpu.CompilerParams(vmem_limit_bytes=32 * 2**20),
    )(grid.where, *weights)


def route_kernel(Z, U, Y, where, *refs):
    near, outs = refs[:Y], refs[Y:]
    z, y = where[0], where[2]
    for k in range(Z):
        target = lax.rem(z + k, Z)
        u = lax.rem(target, U)
        from_y = lax.rem(y - lax.div(target, U) + Y, Y)
        for r in range(Y):

            @pl.when(from_y == r)
            def _(k=k, r=r, u=u):
                outs[k][...] = near[r][u]


def route_heads(grid, near):
    _, half, n = near[0].shape
    return pl.pallas_call(
        functools.partial(route_kernel, grid.Z, grid.U, grid.Y),
        out_shape=[jax.ShapeDtypeStruct((half, n), BF16)] * grid.Z,
        in_specs=[pl.BlockSpec(memory_space=pltpu.SMEM)] + [whole_vmem()] * grid.Y,
        out_specs=[whole_vmem()] * grid.Z,
        compiler_params=pltpu.CompilerParams(vmem_limit_bytes=32 * 2**20),
    )(grid.where, *near)


def assemble_kernel(Z, X, Y, where, *refs):
    units, out = refs[: X * Y], refs[X * Y]
    z, x, y = where[0], where[1], where[2]
    for yr in range(Y):
        for xr in range(X):
            for k in range(Z):
                spot = lax.rem(z - k + Z, Z) * X + lax.rem(x - xr + X, X)
                spot = spot * Y + lax.rem(y - yr + Y, Y)
                out[spot] = units[yr * X + xr][k]


def assemble(grid, units):
    Z, X, Y = grid.Z, grid.X, grid.Y
    _, part, n = units[0].shape
    out = pl.pallas_call(
        functools.partial(assemble_kernel, Z, X, Y),
        out_shape=jax.ShapeDtypeStruct((Z * X * Y, part, n), BF16),
        in_specs=[pl.BlockSpec(memory_space=pltpu.SMEM)] + [whole_vmem()] * (X * Y),
        out_specs=whole_vmem(),
        compiler_params=pltpu.CompilerParams(vmem_limit_bytes=32 * 2**20),
    )(grid.where, *units)
    return out.reshape(-1, n)


def hidden_kernel(Z, X, tiles, order, where, *refs):
    take = Taker(refs)
    act_refs, grad_refs, units = take(tiles), take(tiles), take(X * Z)
    in_own, in_low, out_own, out_low, both_grads, products = take(6)
    weights, acts, grads, sems = take(4)
    z, x = where[0], where[1]
    rows = units[0].shape[0]
    n = units[0].shape[1] // 3
    tokens = act_refs[0].shape[0]
    own = tokens // Z
    ring = sum(jnp.where(z == value, place, 0) for place, value in enumerate(order))

    def rows_of(s):
        ranked = lax.rem(ring - s + Z, Z)
        at = sum(jnp.where(ranked == place, value, 0) for place, value in enumerate(order))
        return at * own

    copies = []
    for xr in range(X):
        for k in range(Z):
            spot = lax.rem(z - k + Z, Z) * X + lax.rem(x - xr + X, X)
            at = pl.ds(pl.multiple_of(spot * rows, 16), rows)
            copies.append(pltpu.make_async_copy(units[xr * Z + k], weights.at[at], sems.at[0]))
    for i in range(tiles):
        copies.append(pltpu.make_async_copy(act_refs[i], acts.at[i], sems.at[0]))
        for s in range(Z):
            at = pl.ds(pl.multiple_of(rows_of(s), own), own)
            copies.append(
                pltpu.make_async_copy(
                    grad_refs[i].at[at], grads.at[i, pl.ds(s * own, own)], sems.at[0]
                )
            )
    for copy in copies:
        copy.start()
    for copy in copies:
        copy.wait()

    def one_tile(i, carry):
        both = dot(acts[i], weights[:, : 2 * n])
        gate, up = both[:, :n], both[:, n:]
        product_grad = dot(grads[i], weights[:, 2 * n :])
        sigma = 1.0 / (1.0 + jnp.exp(-gate))
        silu = gate * sigma
        product = (silu * up).astype(BF16)
        up_grad = (product_grad * silu).astype(BF16)
        gate_grad = (product_grad * up * sigma * (1.0 + gate * (1.0 - sigma))).astype(BF16)
        both_grad = jnp.concatenate([gate_grad, up_grad], 1)
        at = pl.ds(pl.multiple_of(i * tokens, tokens), tokens)
        both_grads[at, :] = both_grad
        in_part = contract_last(both_grad, weights[:, : 2 * n])
        out_part = contract_last(product, weights[:, 2 * n :])
        for s in range(Z):
            spot = pl.ds(pl.multiple_of(i * tokens + rows_of(s), own), own)
            products[spot, :] = product[s * own : (s + 1) * own]

        @pl.when(i == 0)
        def _():
            in_own[...] = in_part
            for s in range(Z):
                spot = pl.ds(pl.multiple_of(rows_of(s), own), own)
                out_own[spot, :] = out_part[s * own : (s + 1) * own]

        @pl.when(i > 0)
        def _():
            low_at = pl.ds(pl.multiple_of((i - 1) * tokens, tokens), tokens)
            in_low[low_at, :] = in_part.astype(BF16)
            for s in range(Z):
                spot = pl.ds(pl.multiple_of((i - 1) * tokens + rows_of(s), own), own)
                out_low[spot, :] = out_part[s * own : (s + 1) * own].astype(BF16)

        return carry

    lax.fori_loop(0, tiles, one_tile, 0)


def hidden_layer(grid, acts, grads, units):
    Z, X, C = grid.Z, grid.X, grid.C
    tokens, width = acts[0].shape
    n = units[0].shape[1] // 3
    shape = jax.ShapeDtypeStruct
    rows = [shape((tokens, width), F32), shape(((C - 1) * tokens, width), BF16)]
    shapes = rows + rows + [shape((C * tokens, 2 * n), BF16), shape((C * tokens, n), BF16)]
    return pl.pallas_call(
        functools.partial(hidden_kernel, Z, X, C, tuple(grid.order)),
        out_shape=shapes,
        in_specs=[pl.BlockSpec(memory_space=pltpu.SMEM)] + [anywhere()] * (2 * C + X * Z),
        out_specs=[whole_vmem()] * len(shapes),
        scratch_shapes=[
            pltpu.VMEM((width, 3 * n), BF16),
            pltpu.VMEM((C, tokens, width), BF16),
            pltpu.VMEM((C, tokens, width), BF16),
            pltpu.SemaphoreType.DMA((1,)),
        ],
        compiler_params=pltpu.CompilerParams(vmem_limit_bytes=36 * 2**20),
        cost_estimate=pl.CostEstimate(
            flops=12 * C * tokens * width * n,
            bytes_accessed=20 * 2**20,
            transcendentals=C * tokens * n,
        ),
    )(grid.where, *acts, *grads, *units)


def norm_kernel(values, more, gain, total, normed):
    hidden = values[...].astype(F32) + more[...].astype(F32)
    recip = lax.rsqrt(jnp.mean(hidden * hidden, -1, keepdims=True) + EPSILON)
    total[...] = hidden
    normed[...] = (hidden * recip * gain[...]).astype(BF16)


def add_norm(values, more, gain):
    return pl.pallas_call(
        norm_kernel,
        out_shape=[
            jax.ShapeDtypeStruct(values.shape, F32),
            jax.ShapeDtypeStruct(values.shape, BF16),
        ],
        in_specs=[whole_vmem()] * 3,
        out_specs=[whole_vmem()] * 2,
        compiler_params=pltpu.CompilerParams(vmem_limit_bytes=32 * 2**20),
    )(values, more, gain)


def norm_back_kernel(number, *refs):
    parts = refs[:number]
    values, beside, gain, grad, low, gain_term = refs[number:]
    part = parts[0][...].astype(F32)
    for ref in parts[1:]:
        part = part + ref[...].astype(F32)
    value = values[...].astype(F32)
    recip = lax.rsqrt(jnp.mean(value * value, -1, keepdims=True) + EPSILON)
    normal = value * recip
    scaled = part * gain[...]
    mean = jnp.mean(scaled * normal, -1, keepdims=True)
    total = beside[...].astype(F32) + recip * (scaled - normal * mean)
    grad[...] = total
    low[...] = total.astype(BF16)
    gain_term[...] = jnp.sum(part * normal, 0, keepdims=True)


def norm_back(parts, values, beside, gain):
    return pl.pallas_call(
        functools.partial(norm_back_kernel, len(parts)),
        out_shape=[
            jax.ShapeDtypeStruct(values.shape, F32),
            jax.ShapeDtypeStruct(values.shape, BF16),
            jax.ShapeDtypeStruct(gain.shape, F32),
        ],
        in_specs=[whole_vmem()] * (3 + len(parts)),
        out_specs=[whole_vmem()] * 3,
        compiler_params=pltpu.CompilerParams(vmem_limit_bytes=32 * 2**20),
    )(*parts, values, beside, gain)


def order_kernel(Z, C, order, where, *refs):
    pieces, out = refs[:-1], refs[-1]
    own = out.shape[0] // (Z * C)
    z, c = where[0], where[3]
    ring = sum(jnp.where(z == value, place, 0) for place, value in enumerate(order))
    for s in range(Z):
        ranked = lax.rem(ring - s + Z, Z)
        at = sum(jnp.where(ranked == place, value, 0) for place, value in enumerate(order))
        for h in range(C):
            spot = pl.multiple_of((at * C + lax.rem(c - h + C, C)) * own, own)
            out[pl.ds(spot, own), :] = pieces[h][s * own : (s + 1) * own, :]


def order_tokens(grid, pieces):
    tokens, width = pieces[0].shape
    return pl.pallas_call(
        functools.partial(order_kernel, grid.Z, grid.C, tuple(grid.order)),
        out_shape=jax.ShapeDtypeStruct((grid.C * tokens, width), BF16),
        in_specs=[pl.BlockSpec(memory_space=pltpu.SMEM)] + [whole_vmem()] * grid.C,
        out_specs=whole_vmem(),
        compiler_params=pltpu.CompilerParams(vmem_limit_bytes=24 * 2**20),
    )(grid.where, *pieces)


def unit_sum_kernel(number, *refs):
    units, outs = refs[:number], refs[number:]
    for k, out in enumerate(outs):
        total = units[0][k].astype(F32)
        for unit in units[1:]:
            total = total + unit[k].astype(F32)
        out[...] = total.astype(BF16)


def unit_sum(units):
    Z, part, n = units[0].shape
    return pl.pallas_call(
        functools.partial(unit_sum_kernel, len(units)),
        out_shape=[jax.ShapeDtypeStruct((part, n), BF16)] * Z,
        in_specs=[whole_vmem()] * len(units),
        out_specs=[whole_vmem()] * Z,
        compiler_params=pltpu.CompilerParams(vmem_limit_bytes=24 * 2**20),
    )(*units)


def sort_kernel(Z, U, Y, where, *refs):
    parts, outs = refs[:Z], refs[Z:]
    z, y = where[0], where[2]
    for k in range(Z):
        source = lax.rem(z - k + Z, Z)
        ahead = lax.rem(lax.div(source, U) - y + Y, Y)
        for r in range(Y):

            @pl.when(ahead == r)
            def _(k=k, r=r, source=source):
                outs[r][lax.rem(source, U)] = parts[k][...]


def sort_heads(grid, parts):
    half, n = parts[0].shape
    return pl.pallas_call(
        functools.partial(sort_kernel, grid.Z, grid.U, grid.Y),
        out_shape=[jax.ShapeDtypeStruct((grid.U, half, n), BF16)] * grid.Y,
        in_specs=[pl.BlockSpec(memory_space=pltpu.SMEM)] + [whole_vmem()] * grid.Z,
        out_specs=[whole_vmem()] * grid.Y,
        compiler_params=pltpu.CompilerParams(vmem_limit_bytes=24 * 2**20),
    )(grid.where, *parts)


def join_kernel(U, Y, sizes, where, *refs):
    parts, outs = refs[:Y], refs[Y:]
    half = parts[0].shape[1]
    for r in range(Y):
        at = pl.multiple_of(lax.rem(where[2] - r + Y, Y) * half, 8)
        for u in range(U):
            first = 0
            for out, size in zip(outs, sizes):
                columns = parts[r][u, :, first : first + size].astype(F32)
                out[pl.ds(at, half), u * size : (u + 1) * size] = columns
                first += size


def join_heads(grid, parts, sizes):
    U, half, _ = parts[0].shape
    return pl.pallas_call(
        functools.partial(join_kernel, U, grid.Y, sizes),
        out_shape=[jax.ShapeDtypeStruct((grid.Y * half, U * size), F32) for size in sizes],
        in_specs=[pl.BlockSpec(memory_space=pltpu.SMEM)] + [whole_vmem()] * grid.Y,
        out_specs=[whole_vmem()] * len(sizes),
        compiler_params=pltpu.CompilerParams(vmem_limit_bytes=24 * 2**20),
    )(grid.where, *parts)


def place_kernel(Y, C, where, *refs):
    parts, out = refs[:-1], refs[-1]
    y, c = where[2], where[3]
    own = parts[0].shape[0]
    for i, part in enumerate(parts):
        at = lax.rem(c - i // Y + C, C) * own
        at = pl.ds(pl.multiple_of(at, own), own)
        out[lax.rem(y - i % Y + Y, Y), at, :] = part[...].astype(F32)


def place_rows(grid, parts):
    own, width = parts[0].shape
    return pl.pallas_call(
        functools.partial(place_kernel, grid.Y, grid.C),
        out_shape=jax.ShapeDtypeStruct((grid.Y, grid.C * own, width), F32),
        in_specs=[pl.BlockSpec(memory_space=pltpu.SMEM)] + [whole_vmem()] * len(parts),
        out_specs=whole_vmem(),
        compiler_params=pltpu.CompilerParams(vmem_limit_bytes=32 * 2**20),
    )(grid.where, *parts)


def core_sum_kernel(number, own, *refs):
    lows, outs = refs[:number], refs[number:]
    total = own[...]
    for low in lows:
        total = total + low[...].astype(F32)
    if len(outs) == 1:
        outs[0][...] = total.astype(outs[0].dtype)
        return
    half = total.shape[0] // 2
    outs[0][...] = total[:half].astype(outs[0].dtype)
    outs[1][...] = total[half:].astype(outs[1].dtype)


def core_sum(own, lows, kind, pieces):
    rows, width = own.shape
    return pl.pallas_call(
        functools.partial(core_sum_kernel, len(lows)),
        out_shape=[jax.ShapeDtypeStruct((rows // pieces, width), kind)] * pieces,
        in_specs=[whole_vmem()] * (1 + len(lows)),
        out_specs=[whole_vmem()] * pieces,
        compiler_params=pltpu.CompilerParams(vmem_limit_bytes=32 * 2**20),
    )(own, *lows)


def hidden_weight_kernel(X, tiles, where, *refs):
    take = Taker(refs)
    acts, grads = take(tiles), take(tiles)
    Y = (len(refs) - 2 * tiles - X - 1) // 2
    both_grads, products, outs, total = take(Y), take(Y), take(X), take(1)[0]
    x = where[1]
    tokens = acts[0].shape[0]
    rows = outs[0].shape[0]
    n = products[0].shape[1]

    def summed(parts, values):
        sums = None
        for i in range(tiles):
            at = i // Y * tokens
            part = contract_first(parts[i][...], values[i % Y][at : at + tokens, :])
            sums = part if sums is None else sums + part
        return sums

    total[:, : 2 * n] = summed(acts, both_grads)
    total[:, 2 * n :] = summed(grads, products)
    for xr in range(X):
        at = pl.ds(pl.multiple_of(lax.rem(x + xr, X) * rows, 8), rows)
        outs[xr][...] = total[at, :].astype(BF16)


def hidden_weight_grad(grid, k, acts, grads, both_grads, products):
    Z, X, tiles = grid.Z, grid.X, len(acts)
    tokens, width = acts[0].shape
    n = products[0].shape[1]
    block = width // Z

    def features(i, s):
        return (0, lax.rem(s[0] + k, Z))

    return pl.pallas_call(
        functools.partial(hidden_weight_kernel, X, tiles),
        out_shape=[jax.ShapeDtypeStruct((block // X, 3 * n), BF16)] * X,
        grid_spec=pltpu.PrefetchScalarGridSpec(
            num_scalar_prefetch=1,
            grid=(1,),
            in_specs=[pl.BlockSpec((tokens, block), features)] * (2 * tiles)
            + [pl.BlockSpec(value.shape, lambda i, s: (0, 0)) for value in both_grads + products],
            out_specs=[pl.BlockSpec((block // X, 3 * n), lambda i, s: (0, 0))] * X,
            scratch_shapes=[pltpu.VMEM((block, 3 * n), F32)],
        ),
        compiler_params=pltpu.CompilerParams(vmem_limit_bytes=26 * 2**20),
        cost_estimate=pl.CostEstimate(
            flops=6 * tiles * tokens * block * n, bytes_accessed=10 * 2**20, transcendentals=0
        ),
    )(grid.where, *acts, *grads, *both_grads, *products)


def weight_kernel(X, Y, where, act, grad, *refs):
    outs, total = refs[: Y * X], refs[Y * X]
    x, y = where[1], where[2]
    part = outs[0].shape[1]
    total[...] = contract_first(act[...], grad[...])
    for xr in range(X):
        for yr in range(Y):
            at = (lax.rem(x + xr, X) * Y + lax.rem(y + yr, Y)) * part
            at = pl.ds(pl.multiple_of(at, 8), part)
            outs[yr * X + xr][0] = total[at, :].astype(BF16)


def weight_grad(grid, act, grad):
    Z, X, Y = grid.Z, grid.X, grid.Y
    tokens, width = act.shape
    n = grad.shape[1]
    part = width // (Z * X * Y)
    return pl.pallas_call(
        functools.partial(weight_kernel, X, Y),
        out_shape=[jax.ShapeDtypeStruct((Z, part, n), BF16)] * (Y * X),
        grid_spec=pltpu.PrefetchScalarGridSpec(
            num_scalar_prefetch=1,
            grid=(Z,),
            in_specs=[
                pl.BlockSpec((tokens, width // Z), lambda k, s: (0, lax.rem(s[0] + k, Z))),
                pl.BlockSpec((tokens, n), lambda k, s: (0, 0)),
            ],
            out_specs=[pl.BlockSpec((1, part, n), lambda k, s: (k, 0, 0))] * (Y * X),
            scratch_shapes=[pltpu.VMEM((width // Z, n), F32)],
        ),
        compiler_params=pltpu.CompilerParams(vmem_limit_bytes=26 * 2**20),
        cost_estimate=pl.CostEstimate(
            flops=2 * tokens * width * n, bytes_accessed=2 * width * n, transcendentals=0
        ),
    )(grid.where, act, grad)


def identity(number):
    row = lax.broadcasted_iota(jnp.int32, (number, number), 0)
    column = lax.broadcasted_iota(jnp.int32, (number, number), 1)
    return jnp.where(row == column, 1.0, 0.0).astype(BF16)


def visible(X, rows, where, limit, first, tile, keys):
    x = where[1]
    key = lax.broadcasted_iota(jnp.int32, (keys, 1), 0)
    tokens = keys // X
    inside = lax.rem(key, tokens)
    key_x = lax.rem(x - lax.div(key, tokens) + X, X)
    key_pos = (lax.div(inside, rows) * X + key_x) * rows + lax.rem(inside, rows)
    query = first + lax.broadcasted_iota(jnp.int32, (1, tile), 1)
    query_pos = (lax.div(query, rows) * X + x) * rows + lax.rem(query, rows)
    return (key_pos <= query_pos) | (key_pos < limit)


def split_heads(qkv, others, queries, keys_values, turned, group):
    tokens = qkv.shape[0]
    for g in range(group):
        queries[g] = qkv[:, g * HEAD_DIM : (g + 1) * HEAD_DIM]
    eye = identity(2 * HEAD_DIM)
    for i in range(1 + len(others)):
        at = slice(i * tokens, (i + 1) * tokens)
        both = qkv[:, group * HEAD_DIM : (group + 2) * HEAD_DIM] if i == 0 else others[i - 1][...]
        keys_values[0, at, :] = both[:, :HEAD_DIM]
        keys_values[1, at, :] = both[:, HEAD_DIM:]
        turned[:, at] = contract_last(eye, both).astype(BF16)


def attend_kernel(X, rows, group, tile, where, prefix, qkv, *refs):
    take = Taker(refs)
    others, heads, stats = take(X - 1), take(1)[0], take(1)[0]
    queries, keys_values, turned = take(3)
    tokens = qkv.shape[0]
    scale = HEAD_DIM ** (-0.5)
    split_heads(qkv, others, queries, keys_values, turned, group)
    limit = prefix[where[2]]
    for t in range(tokens // tile):
        at = slice(t * tile, (t + 1) * tile)
        allowed = visible(X, rows, where, limit, t * tile, tile, X * tokens)
        outs = []
        for g in range(group):
            scores = contract_last(keys_values[0], queries[g, at, :]) * scale
            scores = jnp.where(allowed, scores, NEGATIVE)
            top = jnp.max(scores, 0, keepdims=True)
            expo = jnp.exp(scores - top)
            total = jnp.sum(expo, 0, keepdims=True)
            probs = (expo / total).astype(BF16)
            outs.append(jnp.transpose(dot(turned[HEAD_DIM:, :], probs)).astype(BF16))
            stats[g : g + 1, at] = top
            stats[group + g : group + g + 1, at] = total
        heads[at, :] = jnp.concatenate(outs, 1)


def attend_back_kernel(X, rows, group, tile, where, prefix, qkv, *refs):
    take = Taker(refs)
    others, heads_grad, stats = take(X - 1), take(1)[0], take(1)[0]
    query_grad, kv_grads = take(1)[0], take(X)
    queries, keys_values, turned, grads, key_sum, value_sum = take(6)
    tokens = qkv.shape[0]
    scale = HEAD_DIM ** (-0.5)
    split_heads(qkv, others, queries, keys_values, turned, group)
    for g in range(group):
        grads[g] = heads_grad[:, g * HEAD_DIM : (g + 1) * HEAD_DIM]
    limit = prefix[where[2]]
    for t in range(tokens // tile):
        at = slice(t * tile, (t + 1) * tile)
        allowed = visible(X, rows, where, limit, t * tile, tile, X * tokens)
        outs = []
        for g in range(group):
            query, grad = queries[g, at, :], grads[g, at, :]
            scores = contract_last(keys_values[0], query) * scale
            scores = jnp.where(allowed, scores, NEGATIVE)
            probs = jnp.exp(scores - stats[g : g + 1, at]) / stats[group + g : group + g + 1, at]
            prob_grad = contract_last(keys_values[1], grad)
            mean = jnp.sum(probs * prob_grad, 0, keepdims=True)
            score_grad = (probs * (prob_grad - mean)).astype(BF16)
            out = jnp.transpose(dot(turned[:HEAD_DIM, :], score_grad)) * scale
            outs.append(out.astype(BF16))
            key_part = dot(score_grad, query)
            value_part = dot(probs.astype(BF16), grad)
            if t == 0 and g == 0:
                key_sum[...] = key_part
                value_sum[...] = value_part
            else:
                key_sum[...] += key_part
                value_sum[...] += value_part
        query_grad[at, :] = jnp.concatenate(outs, 1)
    for i, out in enumerate(kv_grads):
        at = slice(i * tokens, (i + 1) * tokens)
        out[:, :HEAD_DIM] = (key_sum[at, :] * scale).astype(out.dtype)
        out[:, HEAD_DIM:] = value_sum[at, :].astype(out.dtype)


def query_tile(tokens, keys):
    tile = tokens
    while tile > 128 and tile * keys > 2**19:
        tile = tile // 2
    return tile


def attend(grid, rows, group, prefix, qkv, others):
    tokens, keys = qkv.shape[0], grid.X * qkv.shape[0]
    smem = pl.BlockSpec(memory_space=pltpu.SMEM)
    return pl.pallas_call(
        functools.partial(attend_kernel, grid.X, rows, group, query_tile(tokens, keys)),
        out_shape=[
            jax.ShapeDtypeStruct((tokens, group * HEAD_DIM), BF16),
            jax.ShapeDtypeStruct((2 * group, tokens), F32),
        ],
        in_specs=[smem, smem] + [whole_vmem()] * grid.X,
        out_specs=[whole_vmem()] * 2,
        scratch_shapes=[
            pltpu.VMEM((group, tokens, HEAD_DIM), BF16),
            pltpu.VMEM((2, keys, HEAD_DIM), BF16),
            pltpu.VMEM((2 * HEAD_DIM, keys), BF16),
        ],
        compiler_params=pltpu.CompilerParams(vmem_limit_bytes=36 * 2**20),
        cost_estimate=pl.CostEstimate(
            flops=8 * group * tokens * keys * 128,
            bytes_accessed=4 * 2**20,
            transcendentals=group * tokens * keys,
        ),
    )(grid.where, prefix, qkv, *others)


def attend_back(grid, rows, group, prefix, qkv, others, heads_grad, stats):
    tokens, keys = qkv.shape[0], grid.X * qkv.shape[0]
    smem = pl.BlockSpec(memory_space=pltpu.SMEM)
    return pl.pallas_call(
        functools.partial(attend_back_kernel, grid.X, rows, group, query_tile(tokens, keys)),
        out_shape=[jax.ShapeDtypeStruct((tokens, group * HEAD_DIM), BF16)]
        + [jax.ShapeDtypeStruct((tokens, 2 * HEAD_DIM), F32)]
        + [jax.ShapeDtypeStruct((tokens, 2 * HEAD_DIM), BF16)] * (grid.X - 1),
        in_specs=[smem, smem] + [whole_vmem()] * (grid.X + 2),
        out_specs=[whole_vmem()] * (1 + grid.X),
        scratch_shapes=[
            pltpu.VMEM((group, tokens, HEAD_DIM), BF16),
            pltpu.VMEM((2, keys, HEAD_DIM), BF16),
            pltpu.VMEM((2 * HEAD_DIM, keys), BF16),
            pltpu.VMEM((group, tokens, HEAD_DIM), BF16),
            pltpu.VMEM((keys, HEAD_DIM), F32),
            pltpu.VMEM((keys, HEAD_DIM), F32),
        ],
        compiler_params=pltpu.CompilerParams(vmem_limit_bytes=36 * 2**20),
        cost_estimate=pl.CostEstimate(
            flops=16 * group * tokens * keys * 128,
            bytes_accessed=4 * 2**20,
            transcendentals=group * tokens * keys,
        ),
    )(grid.where, prefix, qkv, *others, heads_grad, stats)


class Grid:
    def __init__(self, dp, tensor, seqs, kv_local):
        self.Y = seqs
        self.C = tensor // seqs
        self.U = kv_local
        self.Z = seqs * kv_local
        self.X = dp // self.Z
        assert self.C * self.Y == tensor and self.X * self.Z == dp
        i, j = lax.axis_index("dp"), lax.axis_index("tensor")
        self.z, self.x = i // self.X, i % self.X
        self.y, self.c = j // self.C, j % self.C
        self.where = jnp.stack([self.z, self.x, self.y, self.c]).astype(jnp.int32)
        order = list(range(0, self.Z, 2)) + list(range(1, self.Z, 2))[::-1]
        self.order = order
        self.ring = [order.index(z) for z in range(self.Z)]

    def move(self, value, target):
        pairs = []
        for z in range(self.Z):
            for x in range(self.X):
                for y in range(self.Y):
                    for c in range(self.C):
                        tz, tx, ty, tc = target(z, x, y, c)
                        here = ((z * self.X + x) * self.Y + y) * self.C + c
                        there = ((tz * self.X + tx) * self.Y + ty) * self.C + tc
                        pairs.append((here, there))
        return lax.ppermute(value, AXES, pairs)

    def to_z(self, value, k):
        return self.move(value, lambda z, x, y, c: ((z + k) % self.Z, x, y, c))

    def hop_z(self, value, k):
        if 1 < k < self.Z - 1:
            return self.to_z(self.to_z(value, 1), k - 1)
        return self.to_z(value, k)

    def to_x(self, value, k):
        return self.move(value, lambda z, x, y, c: (z, (x + k) % self.X, y, c))

    def to_y(self, value, k):
        return self.move(value, lambda z, x, y, c: (z, x, (y + k) % self.Y, c))

    def to_c(self, value, k):
        return self.move(value, lambda z, x, y, c: (z, x, y, (c + k) % self.C))

    def along_ring(self, value, k):
        return self.move(
            value, lambda z, x, y, c: (self.order[(self.ring[z] + k) % self.Z], x, y, c)
        )

    def slot_z(self, s):
        place_of = sum(jnp.where(self.z == z, ring, 0) for z, ring in enumerate(self.ring))
        place_of = (place_of - s) % self.Z
        return sum(jnp.where(place_of == at, z, 0) for at, z in enumerate(self.order))

    def to_xy(self, value, kx, ky):
        return self.move(
            value, lambda z, x, y, c: (z, (x + kx) % self.X, (y + ky) % self.Y, c)
        )

    def groups(self, names):
        sizes = {"z": self.Z, "x": self.X, "y": self.Y, "c": self.C}
        members = {}
        for z in range(self.Z):
            for x in range(self.X):
                for y in range(self.Y):
                    for c in range(self.C):
                        at = {"z": z, "x": x, "y": y, "c": c}
                        key = tuple(at[name] for name in sizes if name not in names)
                        rank = 0
                        for name in names:
                            rank = rank * sizes[name] + at[name]
                        index = ((z * self.X + x) * self.Y + y) * self.C + c
                        members.setdefault(key, {})[rank] = index
        return [[group[rank] for rank in range(len(group))] for group in members.values()]

    def gather(self, own, names):
        return lax.all_gather(own, AXES, axis=0, tiled=True, axis_index_groups=self.groups(names))

    def scatter(self, partial, names):
        return lax.psum_scatter(
            partial,
            AXES,
            scatter_dimension=0,
            tiled=True,
            axis_index_groups=self.groups(names),
        )

    def ring_steps(self, own, steps):
        blocks = [own]
        for _ in range(steps):
            blocks.append(self.along_ring(blocks[-1], 1))
        return blocks

    def spread_yc(self, mine):
        pieces = [mine] + [self.to_y(mine, k) for k in range(1, self.Y)]
        return pieces + [self.to_c(piece, k) for k in range(1, self.C) for piece in pieces]

    def gather_wide(self, blocks, hold=()):
        half = self.Z // 2
        first = jnp.concatenate(blocks[:half], 0)
        second = jnp.concatenate(blocks[half:], 0)
        pieces = [jnp.concatenate([first, second], 0)]
        for k in range(1, self.Y):
            pieces.append(
                jnp.concatenate([after(self.to_y(first, k), *hold), self.to_y(second, k)], 0)
            )
        return pieces + [self.to_c(piece, k) for k in range(1, self.C) for piece in pieces]

    def ring_sum(self, slots, holds=()):
        total = slots[-1].astype(BF16)
        for i, s in enumerate(range(self.Z - 2, -1, -1)):
            if i < len(holds):
                total = after(total, *holds[i])
            arrived = self.along_ring(total, -1)
            total = arrived.astype(F32) + slots[s]
            if s > 0:
                total = total.astype(BF16)
        return arrived, slots[0]

    def exchange_z(self, parts):
        return [parts[0]] + [self.to_z(parts[k], k) for k in range(1, self.Z)]

    def spread_xy(self, unit):
        return [
            unit if xr == yr == 0 else self.to_xy(unit, xr, yr)
            for yr in range(self.Y)
            for xr in range(self.X)
        ]

    def send_xy(self, units):
        return [
            unit if i == 0 else self.to_xy(unit, i % self.X, i // self.X)
            for i, unit in enumerate(units)
        ]

    def return_heads(self, parts, sizes):
        sorted_parts = sort_heads(self, parts)
        arrived = [sorted_parts[0]] + [self.to_y(sorted_parts[r], r) for r in range(1, self.Y)]
        return join_heads(self, arrived, sizes)

    def from_z(self, k):
        return (self.z - k) % self.Z

    def spread_x(self, unit):
        parts = [unit] + [self.to_x(unit, k) for k in range(1, self.X)]
        return place(parts, [(self.x - k) % self.X for k in range(self.X)])

    def gather_gains(self, gains):
        xs = self.spread_x(gains)
        parts = [xs] + [self.to_z(xs, k) for k in range(1, self.Z)]
        whole = place(parts, [self.from_z(k) for k in range(self.Z)])
        return whole.transpose(2, 0, 1, 3).reshape(gains.shape[0], -1)

    def sum_gains(self, terms, hold):
        number = terms.shape[0]
        part = terms
        for k in range(1, self.C):
            part = part + self.to_c(terms, k)
        terms = part
        for k in range(1, self.Y):
            part = part + self.to_y(terms, k)
        part = after(part, *hold)
        part = part.reshape(number, self.Z, self.X, -1).transpose(2, 1, 0, 3)
        out = pick(part, self.x)
        for k in range(1, self.X):
            out = out + self.to_x(pick(part, (self.x + k) % self.X), k)
        return sum(self.exchange_z([pick(out, (self.z + k) % self.Z) for k in range(self.Z)]))


def per_device(
    dp,
    tensor,
    inputs,
    cotangent,
    prefix,
    gain_attn,
    w_query,
    w_key,
    w_value,
    w_out,
    gain_mlp,
    w_gate,
    w_up,
    w_down,
):
    seqs, rows, width = inputs.shape
    kv_local = w_key.shape[1] // HEAD_DIM
    group = w_query.shape[1] // w_key.shape[1]
    grid = Grid(dp, tensor, seqs, kv_local)
    own = rows // grid.C
    q_cols = group * HEAD_DIM

    def own_rows(value):
        return lax.dynamic_slice(value, (grid.y, grid.c * own, 0), (1, own, width))[0]

    others = range(1, grid.X)
    middle = grid.Z // 2
    ends = [k for k in range(1, grid.Z) if k != middle]
    cot_own = own_rows(cotangent)
    cot_all = grid.gather(cot_own, "z")
    near = pack_heads(grid, [after(w_query, cot_own), w_key, w_value])
    near_own = near[0]
    near = [near_own] + [grid.to_y(near[k], k) for k in range(1, grid.Y)]
    gains = grid.gather_gains(jnp.stack([after(gain_attn, cot_own), gain_mlp], 0))
    flat = own_rows(inputs)
    gain_one, gain_two = gains[0:1].astype(F32), gains[1:2].astype(F32)
    values = flat.astype(F32)
    recip = lax.rsqrt(jnp.mean(values * values, -1, keepdims=True) + EPSILON)
    attn_own = after((values * recip * gain_one).astype(BF16), *near)
    qkv_parts = grid.exchange_z(route_heads(grid, near))

    packed = pack_hidden(grid, after(w_gate, attn_own), w_up, w_down.T)
    out_near = pack_heads(grid, [after(w_out.T, packed[0])])
    out_near = [out_near[0]] + [grid.to_y(out_near[k], k) for k in range(1, grid.Y)]

    def ring_on(blocks, *hold):
        return blocks + [grid.along_ring(after(blocks[-1], *hold), 1)]

    blocks = ring_on([attn_own])
    blocks = ring_on(blocks, *packed[:1])
    blocks = ring_on(blocks, *qkv_parts, *[cot_all])
    for _ in range(grid.Z - 4):
        blocks = ring_on(blocks)
    qkv_units = grid.spread_xy(jnp.stack(qkv_parts, 0))
    out_parts = route_heads(grid, [after(part, *qkv_parts) for part in out_near])
    out_parts = grid.exchange_z(out_parts)
    mine = after(jnp.concatenate(blocks, 0), *qkv_units[1:], *out_parts[1:])
    attn_in = order_tokens(grid, [mine] + [grid.to_c(mine, k) for k in range(1, grid.C)])

    w_qkv = assemble(grid, qkv_units)
    w_qkv = w_qkv[:, : q_cols + 2 * HEAD_DIM]
    qkv = dot(attn_in, w_qkv).astype(BF16)
    tokens = qkv.shape[0]
    kv_own = qkv[:, q_cols:]
    kv_others = [grid.to_x(kv_own, k) for k in others]
    out_units = grid.spread_xy(after(jnp.stack(out_parts, 0), *qkv_units[1:]))
    w_o = assemble(grid, out_units)[:, :q_cols]
    arrived, first, hop = {0: packed[0]}, out_parts[1:], []
    for k in [middle] + ends:
        part = after(packed[k], *first)
        if k == middle and middle > 1:
            hop = [grid.to_z(part, 1)]
            arrived[k] = grid.to_z(after(hop[0], *out_units[1:]), middle - 1)
        else:
            arrived[k] = grid.to_z(part, k)
        first = [arrived[k]]
    ready = after(qkv, *out_units[1:], *hop)
    heads, stats = attend(grid, rows, group, prefix, ready, kv_others)
    moved_x, first = {}, out_units[1:]
    for k in [0, middle] + ends:
        moved_x[k] = [grid.to_x(after(arrived[k], *first), x) for x in others]
        first = moved_x[k]
    mlp_grad = grid.spread_yc(after(cot_all, *out_units[1:], *[heads]))
    attn_partial = contract_last(after(heads, *[arrived[middle]]), w_o).astype(BF16)
    attn_out = grid.scatter(attn_partial, "zc")
    held = list(mlp_grad[: grid.Y]) + list([arrived[ends[0]]]) + list(moved_x[middle])
    hidden, mlp_own = add_norm(flat, after(attn_out, *held), gain_two)
    mlp_blocks = ring_on([mlp_own])
    mlp_blocks = ring_on(mlp_blocks)
    for _ in range(grid.Z - 3):
        mlp_blocks = ring_on(mlp_blocks, *[arrived[ends[-1]]])
    mlp_in = grid.gather_wide(mlp_blocks, list(moved_x[ends[-1]]))
    units = [arrived[k] for k in range(grid.Z)]
    units = units + [moved_x[k][x - 1] for x in others for k in range(grid.Z)]

    layers, in_moved, hold = [None] * grid.Y, [], ()
    for yr in range(grid.Y - 1, -1, -1):
        acts = [mlp_in[c * grid.Y + yr] for c in range(grid.C)]
        acts[0] = after(acts[0], *hold)
        grads = [mlp_grad[c * grid.Y + yr] for c in range(grid.C)]
        layers[yr] = hidden_layer(grid, acts, grads, units)
        each = acts[0].shape[0]
        half = each // 2
        low = after(layers[yr][1], *[sent[0] for sent in in_moved])
        moved = [grid.to_c(low[(h - 1) * each : h * each], -h) for h in range(1, grid.C)]
        if yr > 0:
            hold = core_sum(layers[yr][0], moved, BF16, 2)
            in_moved.append([grid.to_y(hold[1], -yr), grid.to_y(hold[0], -yr)])
    both_grads = [layer[4] for layer in layers]
    products = [layer[5] for layer in layers]

    order = [middle] + ends + [0]
    swapped, hidden_parts, holds = [], [None] * grid.Z, []
    for at, k in enumerate(order):
        hold = [in_late] if at else []
        given = both_grads[:-1] + [after(both_grads[-1], *hold)]
        parts = list(hidden_weight_grad(grid, k, mlp_in, mlp_grad, given, products))
        if at == 0:
            in_late, in_first = core_sum(after(layers[0][0], *parts), moved, F32, 2)
        first = swapped[-1] if swapped else []
        swapped.append([grid.to_x(after(parts[xr], *first), xr) for xr in others])
        holds.append(parts)
    for at, k in enumerate(order):
        late = list(holds[1]) + list(holds[2]) if at == 0 else []
        hidden_parts[k] = core_sum(after(holds[at][0], *late), swapped[at], BF16, 1)[0]
    for sent in in_moved:
        in_first = in_first + sent[0].astype(F32)
    in_late = after(in_late, in_first)
    for sent in in_moved:
        in_late = in_late + sent[1].astype(F32)
    slots = [
        (in_late, in_first)[2 * s // grid.Z][s % (grid.Z // 2) * own :][:own]
        for s in range(grid.Z)
    ]
    last = holds[3]
    holds = [
        [],
        list(holds[1]) + list([hidden_parts[middle]]),
        list(holds[2]) + list([hidden_parts[middle]]),
    ]
    in_parts = grid.ring_sum(slots, holds)
    arrived, first, hop = list(hidden_parts), [], None
    for k in order[:-1]:
        part = after(hidden_parts[k], *first)
        if k == middle and middle > 1:
            hop = grid.to_z(part, 1)
            arrived[k] = grid.to_z(hop, middle - 1)
        else:
            arrived[k] = grid.to_z(part, k)
        first = [arrived[k]]
    held = list(swapped[1]) + list(swapped[2]) + list([arrived[middle]])
    held = held
    in_parts = (after(in_parts[0], *held), in_parts[1])
    hidden_grad, hidden_low, gain_two_term = norm_back(in_parts, hidden, cot_own, gain_two)
    out_y, out_sent, moved_out = [], [], [None] * grid.Y
    for yr in range(grid.Y - 1, -1, -1):
        low = after(layers[yr][3], in_parts[0])
        moved_out[yr] = [grid.to_c(low[(h - 1) * each : h * each], -h) for h in range(1, grid.C)]
        if yr > 0:
            out_sent.append(core_sum(layers[yr][2], moved_out[yr], BF16, 1)[0])
            out_y.append(grid.to_y(out_sent[-1], -yr))
    blocks = ring_on([hidden_low])
    blocks = ring_on(blocks, *out_sent, *moved_out[0])
    for _ in range(grid.Z - 3):
        held = list(last) + list(swapped[3])
        held = held
        blocks = ring_on(blocks, *held)
    mine = jnp.concatenate(blocks, 0)
    pieces = [mine] + [grid.to_c(mine, k) for k in range(1, grid.C)]
    held = []
    pieces[-1] = after(pieces[-1], *held)
    attn_grad = order_tokens(grid, pieces)
    out_sum = core_sum(layers[0][2], moved_out[0] + out_y, BF16, 1)[0]
    mlp_out = grid.scatter(after(out_sum, *[attn_grad]), "z")
    heads_grad = dot(attn_grad, w_o).astype(BF16)
    out_units = weight_grad(grid, attn_grad, heads)

    held = list(out_units) + [out_sum]
    heads_grad = after(heads_grad, *held)
    query_grad, *kv_parts = attend_back(
        grid, rows, group, prefix, qkv, kv_others, heads_grad, stats
    )
    kv_moved = [grid.to_x(kv_parts[k], -k) for k in others]
    out_moved = grid.send_xy(out_units)
    held = list(out_moved[1:]) + list([arrived[order[2]]])
    held = held
    kv_grad = after(kv_parts[0], *held)
    for part in kv_moved:
        kv_grad = kv_grad + part.astype(F32)
    qkv_grad = jnp.concatenate(
        [query_grad, kv_grad.astype(BF16)], 1
    )

    def spread_y(value):
        return [value] + [grid.to_y(value, k) for k in range(1, grid.Y)]

    def spread_c(ys):
        cs = [grid.to_c(part, k) for k in range(1, grid.C) for part in ys]
        return place_rows(grid, ys + cs)

    qkv_units = weight_grad(grid, attn_in, qkv_grad)
    qkv_moved = grid.send_xy(qkv_units)
    out_sums = unit_sum([after(unit) for unit in out_moved])
    out_parts = grid.exchange_z(out_sums)
    held = list(qkv_units) + list(out_parts[1:]) + list([arrived[order[2]]])
    held = held
    partial = contract_last(after(qkv_grad, *held), w_qkv).astype(BF16)
    attn_in_grad = grid.scatter(partial, "zc")
    gate_wgrad, up_wgrad, down_wgrad = unpack_hidden(
        grid, [after(part, *[partial]) for part in arrived]
    )
    out_wgrad = grid.return_heads(out_parts, (q_cols,))[0]
    result_low = (hidden + after(mlp_out, *[partial]).astype(F32)).astype(BF16)
    result = spread_c(spread_y(result_low))
    held = [gate_wgrad]
    held = held + list(out_parts[1:])
    qkv_sums = unit_sum([after(unit, *held) for unit in qkv_moved])
    qkv_parts = grid.exchange_z(qkv_sums)
    qkv_wgrad = grid.return_heads(qkv_parts, (q_cols, HEAD_DIM, HEAD_DIM))
    held = list(qkv_sums) + [out_wgrad] + list(qkv_wgrad)
    held = held
    ready = after(attn_in_grad, *held)
    _, input_low, gain_one_term = norm_back([ready], flat, hidden_grad, gain_one)
    input_ys = spread_y(input_low)
    input_grad = spread_c(input_ys)
    gain_sum = grid.sum_gains(
        jnp.concatenate([gain_one_term, gain_two_term], 0),
        [],
    )
    down_wgrad = down_wgrad.T

    return (
        result,
        input_grad,
        gain_sum[0],
        qkv_wgrad[0],
        qkv_wgrad[1],
        qkv_wgrad[2],
        out_wgrad.T,
        gain_sum[1],
        gate_wgrad,
        up_wgrad,
        down_wgrad,
    )


def solution(mesh):
    dp, tensor = mesh.shape["dp"], mesh.shape["tensor"]

    def step(*args):
        return per_device(dp, tensor, *args)

    return jax.shard_map(
        step,
        mesh=mesh,
        in_specs=(
            P(None, "dp", None),
            P(None, "dp", None),
            P(),
            P("dp"),
            P("dp", "tensor"),
            P("dp", "tensor"),
            P("dp", "tensor"),
            P("tensor", "dp"),
            P("dp"),
            P("dp", "tensor"),
            P("dp", "tensor"),
            P("tensor", "dp"),
        ),
        out_specs=(
            P(None, "dp", None),
            P(None, "dp", None),
            P("dp"),
            P("dp", "tensor"),
            P("dp", "tensor"),
            P("dp", "tensor"),
            P("tensor", "dp"),
            P("dp"),
            P("dp", "tensor"),
            P("dp", "tensor"),
            P("tensor", "dp"),
        ),
        check_vma=False,
    )
```
